256 devices in a mesh: ctx: 32 (over x_hi, z, core), dp: 8 (over x_lo, y).
Axes of the slice: x: 4 (x_hi: 2, x_lo: 2; x = x_hi * 2 + x_lo), y: 4, z: 8, core: 2. Of those that a mesh axis runs over, the one named last changes fastest.
Arguments:
- q_raw: bfloat16 [8, 8192, 2048], P('dp', 'ctx')
- raw_keys_input: bfloat16 [8, 8192, 1024], P('dp', 'ctx')
- values: bfloat16 [8, 8192, 1024], P('dp', 'ctx'), may hold values from -6 to 6
- grad_out: bfloat16 [8, 8192, 2048], P('dp', 'ctx')
- q_gain: float32 [128], replicated
- k_gain: float32 [128], replicated, may hold values from 0.5 to 1.5
- doc_starts: int32 [8, 4], P('dp'), may hold values from 1 to 8191, as said below
- flags: int32 [8, 32], P('dp'), may hold values 0 or 1
Outputs:
- dq_raw: bfloat16 [8, 8192, 2048], P('dp', 'ctx')
- raw_key_gradient: bfloat16 [8, 8192, 1024], P('dp', 'ctx')
- dvalues: bfloat16 [8, 8192, 1024], P('dp', 'ctx')
- dq_gain: float32 [128], replicated
- dk_gain: float32 [128], replicated
The draws below stay inside these ranges and needn't reach their ends.
Inputs may be any that keep to these rules, and one draw needn't show every extreme that they name: `doc_starts`: each row lists 4 distinct offsets in increasing order.
All inputs are finite; a program needn't handle non-finite values. No bound on the sum of `flags` on one device may be relied on, other than what follows from the above.
Results may differ from the reference program's by a relative error of at most 0.004.
The reference program's roundings to bfloat16 on the way count: a program that leaves them out, or rounds other values in their place, can miss the bound.
Values may be sent and summed in bfloat16 or wider, within the bound.
No kernel may reach another device: no remote copies, remote signals or barrier semaphores. Data moves between devices by JAX's collectives and lax.ppermute only.
A program may use at most 128 MiB of HBM per device.

```python
import jax
import jax.numpy as jnp
from jax import lax

QUERY_HEADS = 16
KEY_VALUE_HEADS = 8
HEAD_SIZE = 128
WINDOW = 1024
DEVICE_TOKENS = 256
DOCS = 4
HOPS = 4
SEQUENCE_COUNT = 8
CTX_SHARDS = 32
SEQUENCE_TOKENS = 8192


def joint_fields(key, strength):
    base_keys = jax.random.normal(jax.random.fold_in(key, 2), (SEQUENCE_COUNT, SEQUENCE_TOKENS, KEY_VALUE_HEADS, HEAD_SIZE), jnp.float32)
    base_q = jax.random.normal(jax.random.fold_in(key, 1), (SEQUENCE_COUNT, SEQUENCE_TOKENS, QUERY_HEADS, HEAD_SIZE), jnp.float32)
    key_offset = jax.random.uniform(jax.random.fold_in(key, 4), (SEQUENCE_COUNT, SEQUENCE_TOKENS, KEY_VALUE_HEADS, HEAD_SIZE), jnp.float32, -1.7, 1.7)
    random_noise = jax.random.normal(jax.random.fold_in(key, 3), (SEQUENCE_COUNT, SEQUENCE_TOKENS, KEY_VALUE_HEADS, HEAD_SIZE), jnp.float32)
    pos = jnp.arange(SEQUENCE_TOKENS)[None, :, None, None]
    twin = jnp.roll(key_offset, 1, axis=1) + 0.06 * random_noise
    key_rows = jnp.where((pos % 64 == 0) & (pos > 0), twin, key_offset)
    source_device = jnp.repeat(jnp.roll(key_rows, 5, axis=1), QUERY_HEADS // KEY_VALUE_HEADS, axis=2)
    queries = jnp.where(pos % 64 == 5, source_device, base_q)
    picked_q = jnp.where(strength > 0.5, queries, base_q)
    picked_k = jnp.where(strength > 0.5, key_rows, base_keys)
    return (picked_q, picked_k)


def draw_q_raw(key, part):
    queries, key_rows = joint_fields(key, 0.0)
    return queries.reshape(SEQUENCE_COUNT, SEQUENCE_TOKENS, QUERY_HEADS * HEAD_SIZE).astype(jnp.bfloat16)


def draw_raw_keys_input(key, part):
    queries, key_rows = joint_fields(key, 0.0)
    return key_rows.reshape(SEQUENCE_COUNT, SEQUENCE_TOKENS, KEY_VALUE_HEADS * HEAD_SIZE).astype(jnp.bfloat16)


def draw_grad_out(key, part):
    key = jax.random.fold_in(key, 21)
    sequence_index = jnp.arange(SEQUENCE_COUNT, dtype=jnp.float32)[:, None, None]
    pos = jnp.arange(SEQUENCE_TOKENS, dtype=jnp.float32)[None, :, None]
    factor = 1.0 + 2.0 * (sequence_index * SEQUENCE_TOKENS + pos) / (SEQUENCE_COUNT * SEQUENCE_TOKENS - 1.0)
    base = jax.random.normal(key, (SEQUENCE_COUNT, SEQUENCE_TOKENS, QUERY_HEADS * HEAD_SIZE), jnp.float32)
    return (base * factor).astype(jnp.bfloat16)


def draw_q_gain(key, part):
    key = jax.random.fold_in(key, 31)
    gain = jax.random.uniform(key, (HEAD_SIZE,), jnp.float32, 0.5, 1.5)
    return gain


def draw_doc_starts(key, part):
    key = jax.random.fold_in(key, 11)
    row_keys = jax.random.split(jax.random.fold_in(key, 1), SEQUENCE_COUNT)

    def one_row(row_key):
        picked = jax.random.choice(row_key, SEQUENCE_TOKENS - 3, (DOCS,), replace=False) + 2
        return jnp.sort(picked).astype(jnp.int32)
    table = jax.vmap(one_row)(row_keys)
    chosen_row = jax.random.randint(jax.random.fold_in(key, 2), (), 0, SEQUENCE_COUNT)
    row_ids = jnp.arange(SEQUENCE_COUNT, dtype=jnp.int32)[:, None]
    col_ids = jnp.arange(DOCS, dtype=jnp.int32)[None, :]
    table = jnp.where((row_ids == chosen_row) & (col_ids == 0), 1, table)
    table = jnp.where((row_ids == chosen_row) & (col_ids == DOCS - 1), SEQUENCE_TOKENS - 1, table)
    return table.astype(jnp.int32)


def touch_ends(entries, rng, smallest, largest):
    longest = entries.shape.index(max(entries.shape))
    spots = []
    for shift in (0, 1):
        where = [jax.random.randint(jax.random.fold_in(rng, axis), (), 0, length) for axis, length in enumerate(entries.shape)]
        where[longest] = (where[longest] + shift) % entries.shape[longest]
        spots.append(tuple(where))
    return entries.at[spots[0]].set(smallest).at[spots[1]].set(largest)


def levels(key, shape, cuts, low, largest):
    factor_of, own = 1.0, jax.random.fold_in(key, 6)
    for dim, parts in cuts:
        steps = jnp.exp(jax.random.uniform(jax.random.fold_in(own, dim), (parts,), jnp.float32, low / len(cuts), largest / len(cuts)))
        factor_of = factor_of * jnp.repeat(steps, shape[dim] // parts).reshape([-1 if axis == dim else 1 for axis in range(len(shape))])
    return factor_of


def scatter_about(key, extent, scale, bound, pieces=(), held_as=jnp.bfloat16):
    drawn = jax.random.normal(key, extent, jnp.float32) * scale
    if len(pieces) > 0:
        drawn = levels(key, extent, pieces, -0.22, 0.18) * drawn
    return jnp.clip(drawn, min=-bound, max=bound).astype(held_as)


def setup_inputs(seed: int = 0) -> dict:
    seeds = jax.random.split(jax.random.key(seed), 9)
    q_raw = draw_q_raw(jax.random.fold_in(seeds[8], 71), 0)
    raw_keys_input = draw_raw_keys_input(jax.random.fold_in(seeds[8], 71), 0)
    values = scatter_about(seeds[2], (SEQUENCE_COUNT, SEQUENCE_TOKENS, KEY_VALUE_HEADS * HEAD_SIZE), 1.0, 6.0, ((0, 8), (1, 32)))
    grad_out = draw_grad_out(jax.random.fold_in(seeds[8], 71), 0)
    q_gain = draw_q_gain(jax.random.fold_in(seeds[8], 71), 0)
    k_gain = jnp.clip(jax.random.uniform(seeds[5], (HEAD_SIZE,), jnp.float32, 0.5, 1.5), 0.5, 1.5)
    doc_starts = draw_doc_starts(jax.random.fold_in(seeds[8], 71), 0)
    flags = touch_ends((jax.random.randint(seeds[7], (SEQUENCE_COUNT, CTX_SHARDS), 0, 8) < 1).astype(jnp.int32), jax.random.fold_in(seeds[7], 1), 0, 1)
    return dict(q_raw=q_raw, raw_keys_input=raw_keys_input, values=values, grad_out=grad_out, q_gain=q_gain, k_gain=k_gain, doc_starts=doc_starts, flags=flags)


query_scale = 168.0 ** (-0.5)
eps = 1e-06

def normalize(x, gain):
    ratio = lax.rsqrt(lax.optimization_barrier(jnp.mean(x * x, axis=-1, keepdims=True)) + eps)
    unit = x * ratio
    return (unit * gain, unit, ratio)

def norm_back(grad, unit, ratio, gain):
    scaled = grad * gain
    dx = ratio * (scaled - unit * lax.optimization_barrier(jnp.mean(scaled * unit, axis=-1, keepdims=True)))
    dgain = lax.optimization_barrier(jnp.sum((grad * unit).reshape(-1, grad.shape[-1]), axis=0))
    return (dx, dgain)

def rounded(x):
    return lax.optimization_barrier(x.astype(jnp.bfloat16)).astype(jnp.float32)

def segment_of(pos, starts, flag_row):
    listed = lax.optimization_barrier(jnp.sum((starts[None, :] <= pos[:, None]).astype(jnp.int32), axis=1))
    heads = jnp.arange(flag_row.shape[0], dtype=jnp.int32) * DEVICE_TOKENS
    flagged = lax.optimization_barrier(jnp.sum(jnp.where(heads[None, :] <= pos[:, None], flag_row[None, :], 0), axis=1))
    return listed + flagged

def head_block(query_block, output_gradient, key_rows, value_rows, allowed):
    qf = query_block.astype(jnp.float32)
    df = output_gradient.astype(jnp.float32)
    kf = key_rows.astype(jnp.float32)
    vf = value_rows.astype(jnp.float32)
    score = jnp.einsum('qgd,kd->gqk', qf, kf) * query_scale
    score = jnp.where(allowed[None], score, -1e+30)
    top = lax.optimization_barrier(jnp.max(score, axis=-1, keepdims=True))
    expo = jnp.exp(score - top)
    prob = expo / lax.optimization_barrier(jnp.sum(expo, axis=-1, keepdims=True))
    probr = rounded(prob)
    outv = jnp.einsum('gqk,kd->qgd', probr, vf)
    delta = lax.optimization_barrier(jnp.sum(df * outv, axis=-1))
    dprob = jnp.einsum('qgd,kd->gqk', df, vf)
    dscore = rounded(prob * (dprob - jnp.transpose(delta)[:, :, None]) * query_scale)
    dvals = jnp.einsum('gqk,qgd->kd', probr, df)
    dquery = jnp.einsum('gqk,kd->qgd', dscore, kf)
    dkeys = jnp.einsum('gqk,qgd->kd', dscore, qf)
    return (dquery, dkeys, dvals)

def reference(q_raw, raw_keys_input, values, grad_out, q_gain, k_gain, doc_starts, flags):
    query_group = QUERY_HEADS // KEY_VALUE_HEADS
    window_span = (HOPS + 1) * DEVICE_TOKENS
    padding_width = HOPS * DEVICE_TOKENS
    qx = q_raw.astype(jnp.float32).reshape(SEQUENCE_COUNT, SEQUENCE_TOKENS, QUERY_HEADS, HEAD_SIZE)
    key_extra = raw_keys_input.astype(jnp.float32).reshape(SEQUENCE_COUNT, SEQUENCE_TOKENS, KEY_VALUE_HEADS, HEAD_SIZE)
    qn_f, q_unit, q_ratio = normalize(qx, q_gain)
    kn_f, k_unit, k_ratio = normalize(key_extra, k_gain)
    normed_query = qn_f.astype(jnp.bfloat16)
    kn = kn_f.astype(jnp.bfloat16)
    value_rows = values.reshape(SEQUENCE_COUNT, SEQUENCE_TOKENS, KEY_VALUE_HEADS, HEAD_SIZE)
    cot = grad_out.reshape(SEQUENCE_COUNT, SEQUENCE_TOKENS, QUERY_HEADS, HEAD_SIZE)
    padded_keys = jnp.pad(kn, ((0, 0), (padding_width, 0), (0, 0), (0, 0)))
    padded_values = jnp.pad(value_rows, ((0, 0), (padding_width, 0), (0, 0), (0, 0)))
    zero_state = jnp.zeros((), jnp.int32)

    def one_shard(step, carry):
        dq_acc, key_gradient_running, value_gradient_running = carry
        sequence_index = (step // CTX_SHARDS).astype(jnp.int32)
        shard = (step % CTX_SHARDS).astype(jnp.int32)
        row_number = (shard * DEVICE_TOKENS).astype(jnp.int32)
        query_block = lax.dynamic_slice(normed_query, (sequence_index, row_number, zero_state, zero_state), (1, DEVICE_TOKENS, QUERY_HEADS, HEAD_SIZE))[0]
        output_gradient = lax.dynamic_slice(cot, (sequence_index, row_number, zero_state, zero_state), (1, DEVICE_TOKENS, QUERY_HEADS, HEAD_SIZE))[0]
        key_rows = lax.dynamic_slice(padded_keys, (sequence_index, row_number, zero_state, zero_state), (1, window_span, KEY_VALUE_HEADS, HEAD_SIZE))[0]
        value_block = lax.dynamic_slice(padded_values, (sequence_index, row_number, zero_state, zero_state), (1, window_span, KEY_VALUE_HEADS, HEAD_SIZE))[0]
        starts = lax.dynamic_index_in_dim(doc_starts, sequence_index, 0, keepdims=False)
        flag_row = lax.dynamic_index_in_dim(flags, sequence_index, 0, keepdims=False)
        qpos = row_number + jnp.arange(DEVICE_TOKENS, dtype=jnp.int32)
        kpos = row_number - padding_width + jnp.arange(window_span, dtype=jnp.int32)
        dist = qpos[:, None] - kpos[None, :]
        allowed = (dist >= 0) & (dist < WINDOW) & (kpos[None, :] >= 0)
        allowed = allowed & (segment_of(qpos, starts, flag_row)[:, None] == segment_of(kpos, starts, flag_row)[None, :])
        query_head = jnp.transpose(query_block.reshape(DEVICE_TOKENS, KEY_VALUE_HEADS, query_group, HEAD_SIZE), (1, 0, 2, 3))
        head_gradient = jnp.transpose(output_gradient.reshape(DEVICE_TOKENS, KEY_VALUE_HEADS, query_group, HEAD_SIZE), (1, 0, 2, 3))
        kh = jnp.transpose(key_rows, (1, 0, 2))
        vh = jnp.transpose(value_block, (1, 0, 2))
        dquery, dkeys, dvals = lax.map(lambda xs: head_block(xs[0], xs[1], xs[2], xs[3], allowed), (query_head, head_gradient, kh, vh))
        dquery = jnp.transpose(dquery, (1, 0, 2, 3)).reshape(1, DEVICE_TOKENS, QUERY_HEADS, HEAD_SIZE)
        dkeys = jnp.transpose(dkeys, (1, 0, 2))
        dvals = jnp.transpose(dvals, (1, 0, 2))
        dkeys = jnp.concatenate([rounded(dkeys[:padding_width]), dkeys[padding_width:]], axis=0)[None]
        dvals = jnp.concatenate([rounded(dvals[:padding_width]), dvals[padding_width:]], axis=0)[None]
        dq_acc = lax.dynamic_update_slice(dq_acc, dquery, (sequence_index, row_number, zero_state, zero_state))
        previous_keys = lax.dynamic_slice(key_gradient_running, (sequence_index, row_number, zero_state, zero_state), (1, window_span, KEY_VALUE_HEADS, HEAD_SIZE))
        key_gradient_running = lax.dynamic_update_slice(key_gradient_running, previous_keys + dkeys, (sequence_index, row_number, zero_state, zero_state))
        previous_values = lax.dynamic_slice(value_gradient_running, (sequence_index, row_number, zero_state, zero_state), (1, window_span, KEY_VALUE_HEADS, HEAD_SIZE))
        value_gradient_running = lax.dynamic_update_slice(value_gradient_running, previous_values + dvals, (sequence_index, row_number, zero_state, zero_state))
        return (dq_acc, key_gradient_running, value_gradient_running)
    initial_state = (jnp.zeros((SEQUENCE_COUNT, SEQUENCE_TOKENS, QUERY_HEADS, HEAD_SIZE), jnp.float32), jnp.zeros((SEQUENCE_COUNT, SEQUENCE_TOKENS + padding_width, KEY_VALUE_HEADS, HEAD_SIZE), jnp.float32), jnp.zeros((SEQUENCE_COUNT, SEQUENCE_TOKENS + padding_width, KEY_VALUE_HEADS, HEAD_SIZE), jnp.float32))
    dq_acc, key_gradient_running, value_gradient_running = lax.fori_loop(0, SEQUENCE_COUNT * CTX_SHARDS, one_shard, initial_state)
    dk_sum = key_gradient_running[:, padding_width:]
    value_gradient_total = value_gradient_running[:, padding_width:]
    dq_x, dq_gain = norm_back(dq_acc, q_unit, q_ratio, q_gain)
    key_gradient_extra, dk_gain = norm_back(dk_sum, k_unit, k_ratio, k_gain)
    dq_raw = dq_x.reshape(SEQUENCE_COUNT, SEQUENCE_TOKENS, QUERY_HEADS * HEAD_SIZE).astype(jnp.bfloat16)
    raw_key_gradient = key_gradient_extra.reshape(SEQUENCE_COUNT, SEQUENCE_TOKENS, KEY_VALUE_HEADS * HEAD_SIZE).astype(jnp.bfloat16)
    dvalues = value_gradient_total.reshape(SEQUENCE_COUNT, SEQUENCE_TOKENS, KEY_VALUE_HEADS * HEAD_SIZE).astype(jnp.bfloat16)
    return (dq_raw, raw_key_gradient, dvalues, dq_gain, dk_gain)
```

```python
import functools

import jax
import jax.numpy as jnp
from jax import lax
from jax.experimental import pallas as pl
from jax.experimental.pallas import tpu as pltpu
from jax.sharding import PartitionSpec as P

QUERY_HEADS = 16
KEY_VALUE_HEADS = 8
D = 128
WINDOW = 1024
T = 256
TC = 2 * T
NKV = 4
CHUNKS = (1, 1, 1, 1)
LOG2E = 1.4426950408889634
SCALE = 168.0 ** (-0.5)
EPS = 1e-06

f32 = jnp.float32
bf16 = jnp.bfloat16
VM = pl.BlockSpec(memory_space=pltpu.VMEM)
SM = pl.BlockSpec(memory_space=pltpu.SMEM)
PARAMS = pltpu.CompilerParams(vmem_limit_bytes=24 * 1024 * 1024)
SMALL = pltpu.CompilerParams(vmem_limit_bytes=12 * 1024 * 1024)
NT = (((1,), (1,)), ((), ()))
NN = (((1,), (0,)), ((), ()))
TN = (((0,), (0,)), ((), ()))


def dot(a, b, dims):
    return lax.dot_general(a, b, dims, preferred_element_type=f32)


def cost(us):
    return pl.CostEstimate(flops=int(us * 1e9), bytes_accessed=int(us * 1e6), transcendentals=0)


def al(x, n):
    return pl.multiple_of(x, n)


def split_kv_kernel(idx, k, v, send):
    other = 1 - idx[0] % 2
    for h in range(NKV):
        cols = pl.ds(al(other * (NKV * D) + h * D, D), D)
        send[:, 2 * h * D : (2 * h + 1) * D] = k[:, cols]
        send[:, (2 * h + 1) * D : (2 * h + 2) * D] = v[:, cols]


def split_kv(idx, k, v):
    return pl.pallas_call(
        split_kv_kernel,
        out_shape=jax.ShapeDtypeStruct((T, 2 * NKV * D), bf16),
        in_specs=[SM, VM, VM],
        out_specs=VM,
        compiler_params=SMALL,
        cost_estimate=cost(1),
        name="split_kv",
    )(idx, k, v)


def join_kv_kernel(idx, k, v, recv, *outs):
    a = idx[0] % 2
    mine = pl.ds(al(a * T, T), T)
    theirs = pl.ds(al((1 - a) * T, T), T)
    h = 0
    for out, n in zip(outs, CHUNKS):
        for i in range(n):
            cols = pl.ds(al(a * (NKV * D) + h * D, D), D)
            out[mine, 2 * i * D : (2 * i + 1) * D] = k[:, cols]
            out[mine, (2 * i + 1) * D : (2 * i + 2) * D] = v[:, cols]
            out[theirs, 2 * i * D : (2 * i + 2) * D] = recv[:, 2 * h * D : (2 * h + 2) * D]
            h += 1


def join_kv(idx, k, v, recv):
    return pl.pallas_call(
        join_kv_kernel,
        out_shape=[jax.ShapeDtypeStruct((TC, 2 * n * D), bf16) for n in CHUNKS],
        in_specs=[SM, VM, VM, VM],
        out_specs=[VM] * len(CHUNKS),
        compiler_params=SMALL,
        cost_estimate=cost(1),
        name="join_kv",
    )(idx, k, v, recv)


def split_q_kernel(idx, q, do, send):
    other = 1 - idx[0] % 2
    w = 2 * NKV * D
    cols = pl.ds(al(other * w, w), w)
    send[:, :w] = q[:, cols]
    send[:, w:] = do[:, cols]


def split_q(idx, q, do):
    return pl.pallas_call(
        split_q_kernel,
        out_shape=jax.ShapeDtypeStruct((T, 4 * NKV * D), bf16),
        in_specs=[SM, VM, VM],
        out_specs=VM,
        compiler_params=SMALL,
        cost_estimate=cost(1.5),
        name="split_q",
    )(idx, q, do)


def join_q_kernel(idx, q, do, recv, qa, doa):
    a = idx[0] % 2
    w = 2 * NKV * D
    mine = pl.ds(al(a * T, T), T)
    theirs = pl.ds(al((1 - a) * T, T), T)
    cols = pl.ds(al(a * w, w), w)
    qa[mine, :] = q[:, cols]
    doa[mine, :] = do[:, cols]
    qa[theirs, :] = recv[:, :w]
    doa[theirs, :] = recv[:, w:]


def join_q(idx, q, do, recv):
    w = 2 * NKV * D
    return pl.pallas_call(
        join_q_kernel,
        out_shape=[jax.ShapeDtypeStruct((TC, w), bf16)] * 2,
        in_specs=[SM, VM, VM, VM],
        out_specs=[VM, VM],
        compiler_params=SMALL,
        cost_estimate=cost(2),
        name="join_q",
    )(idx, q, do, recv)


def unit_of(x):
    r = lax.rsqrt(jnp.mean(x * x, axis=-1, keepdims=True) + EPS)
    return x * r, r


def rows8(x, op):
    return op(x.reshape(x.shape[0] // 8, 8, x.shape[1]), axis=0)


def attn_kernel(
    idx, starts, flags, qg, kg, q, do, kv0, kv1, kv2,
    dq, d2, d1, d0, gains,
    bias, s_scr, dp_scr, pb_scr, ds_scr, kn_scr, qn_scr, do_scr, dk_acc, dv_acc,
):
    step = pl.program_id(0)
    first = (idx[0] // 2) * TC

    jl = lax.broadcasted_iota(jnp.int32, (T, T), 0)
    il = lax.broadcasted_iota(jnp.int32, (T, T), 1)
    late = jl > il

    @pl.when(step == 0)
    def _():
        gains[...] = jnp.zeros_like(gains)
        for qb in range(2):
            base = first + qb * T
            qpos = base + lax.broadcasted_iota(jnp.int32, (1, T), 1)
            lo = jnp.maximum(qpos - (WINDOW - 1), 0)
            for n in range(starts.shape[1]):
                b = starts[0, n]
                lo = jnp.maximum(lo, jnp.where(b <= qpos, b, 0))
            for n in range(flags.shape[1]):
                b = flags[0, n] * (n * T)
                lo = jnp.maximum(lo, jnp.where(b <= qpos, b, 0))
            for t in range(4):
                if t == 0:
                    kpos = jnp.where(late, base - WINDOW + jl, base + jl)
                else:
                    kpos = base - WINDOW + t * T + jl
                bias[qb, t] = jnp.where(kpos >= lo, 0.0, -jnp.inf).astype(f32)

    dkg = jnp.zeros((8, D), f32)
    for b, ref in enumerate((kv2, kv1, kv0)):
        xh, _ = unit_of(ref[:, :D].astype(f32))
        kn_scr[b * TC : (b + 1) * TC, :] = (xh * kg[...]).astype(bf16)
    for qb in range(2):
        for g in range(2):
            x = q[qb * T : (qb + 1) * T, g * D : (g + 1) * D].astype(f32)
            xh, _ = unit_of(x)
            qn_scr[qb, g * T : (g + 1) * T, :] = (xh * qg[...]).astype(bf16)
            do_scr[qb, g * T : (g + 1) * T, :] = do[qb * T : (qb + 1) * T, g * D : (g + 1) * D]

    def keys(kb):
        return kn_scr[kb * T : (kb + 1) * T, :]

    def vals(kb):
        ref = (kv2, kv1, kv0)[kb // 2]
        return ref[(kb % 2) * T : (kb % 2 + 1) * T, D:]

    dqg = jnp.zeros((8, D), f32)
    for qb in range(2):
        for g in range(2):
            lanes = slice(g * T, (g + 1) * T)
            qn = qn_scr[qb, lanes, :]
            dog = do_scr[qb, lanes, :]
            m = None
            for t in range(4):
                s = dot(keys(qb + t), qn, NT)
                if t == 0:
                    s = jnp.where(late, s, dot(keys(qb + 4), qn, NT))
                s = s * (SCALE * LOG2E) + bias[qb, t]
                s_scr[t] = s
                mt = rows8(s, jnp.max)
                m = mt if m is None else jnp.maximum(m, mt)
            m = jnp.max(m, axis=0, keepdims=True)
            el = None
            for t in range(4):
                e = jnp.exp2(s_scr[t] - m)
                s_scr[t] = e
                lt = rows8(e, jnp.sum)
                el = lt if el is None else el + lt
            rl = 1.0 / jnp.sum(el, axis=0, keepdims=True)
            delta = None
            for t in range(4):
                dp = dot(vals(qb + t), dog, NT)
                if t == 0:
                    dp = jnp.where(late, dp, dot(vals(qb + 4), dog, NT))
                dp_scr[t] = dp
                p = s_scr[t] * rl
                s_scr[t] = p
                pb = p.astype(bf16)
                dt = rows8(pb.astype(f32) * dp, jnp.sum)
                delta = dt if delta is None else delta + dt
                if t == 0:
                    pb_scr[0, :, lanes] = jnp.where(late, p, 0.0).astype(bf16)
                    pb_scr[4, :, lanes] = jnp.where(late, 0.0, p).astype(bf16)
                else:
                    pb_scr[t, :, lanes] = pb
            delta = jnp.sum(delta, axis=0, keepdims=True)
            for t in range(4):
                ds = s_scr[t] * (dp_scr[t] - delta) * SCALE
                if t == 0:
                    ds_scr[0, :, lanes] = jnp.where(late, ds, 0.0).astype(bf16)
                    ds_scr[4, :, lanes] = jnp.where(late, 0.0, ds).astype(bf16)
                else:
                    ds_scr[t, :, lanes] = ds.astype(bf16)
            dqn = None
            for t in range(5):
                part = dot(ds_scr[t, :, lanes], keys(qb + t), TN)
                dqn = part if dqn is None else dqn + part
            xh, r = unit_of(q[qb * T : (qb + 1) * T, g * D : (g + 1) * D].astype(f32))
            dqg = dqg + rows8(dqn * xh, jnp.sum)
            dxh = dqn * qg[...]
            dx = r * (dxh - xh * jnp.mean(dxh * xh, axis=-1, keepdims=True))
            dq[qb * T : (qb + 1) * T, g * D : (g + 1) * D] = dx.astype(bf16)
        for t in range(5):
            kb = qb + t
            rows = slice(kb * T, (kb + 1) * T)
            dv = dot(pb_scr[t], do_scr[qb], NN)
            dk = dot(ds_scr[t], qn_scr[qb], NN)
            if qb == 0 or t == 4:
                dv_acc[rows, :] = dv
                dk_acc[rows, :] = dk
            else:
                dv_acc[rows, :] += dv
                dk_acc[rows, :] += dk

    for b, (ref, out) in enumerate(((kv2, d2), (kv1, d1), (kv0, d0))):
        xh, _ = unit_of(ref[:, :D].astype(f32))
        dk = dk_acc[b * TC : (b + 1) * TC, :]
        dkg = dkg + rows8(dk * xh, jnp.sum)
        out[:, :D] = dk.astype(out.dtype)
        out[:, D:] = dv_acc[b * TC : (b + 1) * TC, :].astype(out.dtype)
    gains[0] += dqg
    gains[1] += dkg


def attn(h0, n, idx, starts, flags, qg, kg, q, do, kv0, kv1, kv2):
    col = pl.BlockSpec((TC, 2 * D), lambda i: (0, i))
    qcol = pl.BlockSpec((TC, 2 * D), lambda i: (0, h0 + i))
    full = pl.BlockSpec((1, D), lambda i: (0, 0))
    return pl.pallas_call(
        attn_kernel,
        grid=(n,),
        out_shape=[
            jax.ShapeDtypeStruct((TC, 2 * n * D), bf16),
            jax.ShapeDtypeStruct((TC, 2 * n * D), bf16),
            jax.ShapeDtypeStruct((TC, 2 * n * D), f32),
            jax.ShapeDtypeStruct((TC, 2 * n * D), f32),
            jax.ShapeDtypeStruct((2, 8, D), f32),
        ],
        in_specs=[SM, SM, SM, full, full, qcol, qcol, col, col, col],
        out_specs=[col, col, col, col, pl.BlockSpec((2, 8, D), lambda i: (0, 0, 0))],
        scratch_shapes=[
            pltpu.VMEM((2, 4, T, T), f32),
            pltpu.VMEM((4, T, T), f32),
            pltpu.VMEM((4, T, T), f32),
            pltpu.VMEM((5, T, 2 * T), bf16),
            pltpu.VMEM((5, T, 2 * T), bf16),
            pltpu.VMEM((3 * TC, D), bf16),
            pltpu.VMEM((2, 2 * T, D), bf16),
            pltpu.VMEM((2, 2 * T, D), bf16),
            pltpu.VMEM((3 * TC, D), f32),
            pltpu.VMEM((3 * TC, D), f32),
        ],
        compiler_params=PARAMS,
        cost_estimate=cost(6 * n),
        name="attn",
    )(idx, starts, flags, qg, kg, q, do, kv0, kv1, kv2)


def add_kernel(x, y, out):
    out[...] = (x[...] + y[...].astype(f32)).astype(bf16)


def add_back(d1, r1):
    return pl.pallas_call(
        add_kernel,
        out_shape=jax.ShapeDtypeStruct(r1.shape, bf16),
        in_specs=[VM, VM],
        out_specs=VM,
        compiler_params=SMALL,
        cost_estimate=cost(1),
        name="add_back",
    )(d1, r1)


def finish_kernel(n, idx, kg, d0, r2, kv, keep, send):
    a = idx[0] % 2
    for out, rows in ((keep, pl.ds(al(a * T, T), T)), (send, pl.ds(al((1 - a) * T, T), T))):
        for i in range(n):
            kc = slice(2 * i * D, (2 * i + 1) * D)
            vc = slice((2 * i + 1) * D, (2 * i + 2) * D)
            dk = d0[rows, kc] + r2[rows, kc].astype(f32)
            xh, r = unit_of(kv[rows, kc].astype(f32))
            dxh = dk * kg[...]
            dx = r * (dxh - xh * jnp.mean(dxh * xh, axis=-1, keepdims=True))
            out[:, kc] = dx.astype(bf16)
            out[:, vc] = (d0[rows, vc] + r2[rows, vc].astype(f32)).astype(bf16)


def finish(n, idx, kg, d0, r2, kv):
    return pl.pallas_call(
        functools.partial(finish_kernel, n),
        out_shape=[jax.ShapeDtypeStruct((T, 2 * n * D), bf16)] * 2,
        in_specs=[SM, VM, VM, VM, VM],
        out_specs=[VM, VM],
        compiler_params=SMALL,
        cost_estimate=cost(1),
        name="finish",
    )(idx, kg, d0, r2, kv)


def out_kv_kernel(idx, *refs):
    a = idx[0] % 2
    g = len(CHUNKS)
    keeps, recvs, (dk, dv) = refs[:g], refs[g : 2 * g], refs[2 * g :]
    h = 0
    for keep, recv, n in zip(keeps, recvs, CHUNKS):
        for i in range(n):
            for ref, side in ((keep, a), (recv, 1 - a)):
                cols = pl.ds(al(side * (NKV * D) + h * D, D), D)
                dk[:, cols] = ref[:, 2 * i * D : (2 * i + 1) * D]
                dv[:, cols] = ref[:, (2 * i + 1) * D : (2 * i + 2) * D]
            h += 1


def out_kv(idx, keeps, recvs):
    return pl.pallas_call(
        out_kv_kernel,
        out_shape=[jax.ShapeDtypeStruct((T, KEY_VALUE_HEADS * D), bf16)] * 2,
        in_specs=[SM] + [VM] * (2 * len(CHUNKS)),
        out_specs=[VM, VM],
        compiler_params=SMALL,
        cost_estimate=cost(1),
        name="out_kv",
    )(idx, *keeps, *recvs)


def split_dq_kernel(idx, *refs):
    a = idx[0] % 2
    parts, (send,) = refs[:-1], refs[-1:]
    c = 0
    for part in parts:
        w = part.shape[1]
        send[:, c : c + w] = part[pl.ds(al((1 - a) * T, T), T), :]
        c += w


def split_dq(idx, parts):
    return pl.pallas_call(
        split_dq_kernel,
        out_shape=jax.ShapeDtypeStruct((T, 2 * NKV * D), bf16),
        in_specs=[SM] + [VM] * len(parts),
        out_specs=VM,
        compiler_params=SMALL,
        cost_estimate=cost(1),
        name="split_dq",
    )(idx, *parts)


def out_q_kernel(idx, *refs):
    a = idx[0] % 2
    parts, recv, dq = refs[:-2], refs[-2], refs[-1]
    w = 2 * NKV * D
    c = 0
    for part in parts:
        n = part.shape[1]
        dq[:, pl.ds(al(a * w + c, D), n)] = part[pl.ds(al(a * T, T), T), :]
        c += n
    dq[:, pl.ds(al((1 - a) * w, w), w)] = recv[...]


def out_q(idx, parts, recv):
    return pl.pallas_call(
        out_q_kernel,
        out_shape=jax.ShapeDtypeStruct((T, QUERY_HEADS * D), bf16),
        in_specs=[SM] + [VM] * (len(parts) + 1),
        out_specs=VM,
        compiler_params=SMALL,
        cost_estimate=cost(1),
        name="out_q",
    )(idx, *parts, recv)


def along(x, distance):
    n = lax.axis_size("ctx")
    return lax.ppermute(x, "ctx", [(i, i + distance) for i in range(n) if 0 <= i + distance < n])


def swap(x, axis, bit):
    n = lax.axis_size(axis)
    return lax.ppermute(x, axis, [(i, i ^ bit) for i in range(n)])


def total(x):
    for bit in (1, 2, 4, 8, 16):
        x = x + swap(x, "ctx", bit)
    for bit in (1, 2, 4):
        x = x + swap(x, "dp", bit)
    return x


def on_device(q_raw, raw_keys_input, values, grad_out, q_gain, k_gain, doc_starts, flags):
    idx = lax.axis_index("ctx").astype(jnp.int32).reshape(1)
    q, k, v, do = q_raw[0], raw_keys_input[0], values[0], grad_out[0]
    qg, kg = q_gain.reshape(1, D), k_gain.reshape(1, D)

    kv0 = join_kv(idx, k, v, swap(split_kv(idx, k, v), "ctx", 1))
    qa, doa = join_q(idx, q, do, swap(split_q(idx, q, do), "ctx", 1))
    kv1 = [along(x, 2) for x in kv0]
    kv2 = [along(x, 2) for x in kv1]

    dqs, d1s, d0s, r1s, gains = [], [], [], [], None
    h0 = 0
    for c, n in enumerate(CHUNKS):
        dq, d2, d1, d0, gain = attn(
            h0, n, idx, doc_starts, flags, qg, kg, qa, doa, kv0[c], kv1[c], kv2[c]
        )
        h0 += n
        dqs.append(dq)
        d1s.append(d1)
        d0s.append(d0)
        r1s.append(along(d2, -2))
        gains = gain if gains is None else gains + gain
    keeps, recvs = [], []
    for c, n in enumerate(CHUNKS):
        r2 = along(add_back(d1s[c], r1s[c]), -2)
        keep, send = finish(n, idx, kg, d0s[c], r2, kv0[c])
        keeps.append(keep)
        recvs.append(swap(send, "ctx", 1))
    dk, dv = out_kv(idx, keeps, recvs)
    dq = out_q(idx, dqs, swap(split_dq(idx, dqs), "ctx", 1))
    gain = total(jnp.sum(gains, axis=1))
    return dq[None], dk[None], dv[None], gain[0], gain[1]


def solution(mesh):
    in_specs = (
        P("dp", "ctx", None),
        P("dp", "ctx", None),
        P("dp", "ctx", None),
        P("dp", "ctx", None),
        P(),
        P(),
        P("dp", None),
        P("dp", None),
    )
    out_specs = (P("dp", "ctx", None), P("dp", "ctx", None), P("dp", "ctx", None), P(), P())
    return jax.shard_map(
        on_device, mesh=mesh, in_specs=in_specs, out_specs=out_specs, check_vma=False
    )
```

```python
import functools

import jax
import jax.numpy as jnp
from jax import lax
from jax.experimental import pallas as pl
from jax.experimental.pallas import tpu as pltpu
from jax.sharding import PartitionSpec as P

QUERY_HEADS = 16
KEY_VALUE_HEADS = 8
D = 128
WINDOW = 1024
T = 256
TC = 2 * T
NKV = 4
CHUNKS = (1, 1, 1, 1)
LOG2E = 1.4426950408889634
SCALE = 168.0 ** (-0.5)
EPS = 1e-06

f32 = jnp.float32
bf16 = jnp.bfloat16
VM = pl.BlockSpec(memory_space=pltpu.VMEM)
ANY = pl.BlockSpec(memory_space=pl.ANY)
SM = pl.BlockSpec(memory_space=pltpu.SMEM)
PARAMS = pltpu.CompilerParams(vmem_limit_bytes=24 * 1024 * 1024)
SMALL = pltpu.CompilerParams(vmem_limit_bytes=12 * 1024 * 1024)
NT = (((1,), (1,)), ((), ()))
NN = (((1,), (0,)), ((), ()))
TN = (((0,), (0,)), ((), ()))


def dot(a, b, dims):
    return lax.dot_general(a, b, dims, preferred_element_type=f32)


def cost(us):
    return pl.CostEstimate(flops=int(us * 1e9), bytes_accessed=int(us * 1e6), transcendentals=0)


def al(x, n):
    return pl.multiple_of(x, n)


def split_kv_kernel(idx, k, v, send):
    other = 1 - idx[0] % 2
    for h in range(NKV):
        cols = pl.ds(al(other * (NKV * D) + h * D, D), D)
        send[:, 2 * h * D : (2 * h + 1) * D] = k[:, cols]
        send[:, (2 * h + 1) * D : (2 * h + 2) * D] = v[:, cols]


def split_kv(idx, k, v):
    return pl.pallas_call(
        split_kv_kernel,
        out_shape=jax.ShapeDtypeStruct((T, 2 * NKV * D), bf16),
        in_specs=[SM, VM, VM],
        out_specs=VM,
        compiler_params=SMALL,
        cost_estimate=cost(1),
        name="split_kv",
    )(idx, k, v)


def join_kv_kernel(h0, n, idx, k, v, recv, *rest):
    out = rest[-1]
    a = idx[0] % 2
    mine = pl.ds(al(a * T, T), T)
    theirs = pl.ds(al((1 - a) * T, T), T)
    for i in range(n):
        cols = pl.ds(al(a * (NKV * D) + (h0 + i) * D, D), D)
        out[mine, 2 * i * D : (2 * i + 1) * D] = k[:, cols]
        out[mine, (2 * i + 1) * D : (2 * i + 2) * D] = v[:, cols]
    out[theirs, :] = recv[:, 2 * h0 * D : 2 * (h0 + n) * D]


def join_kv(h0, n, idx, k, v, recv, after):
    return pl.pallas_call(
        functools.partial(join_kv_kernel, h0, n),
        out_shape=jax.ShapeDtypeStruct((TC, 2 * n * D), bf16),
        in_specs=[SM, VM, VM, VM] + [ANY] * len(after),
        out_specs=VM,
        compiler_params=SMALL,
        cost_estimate=cost(0.2),
        name="join_kv",
    )(idx, k, v, recv, *after)


def split_q_kernel(idx, q, do, after, send):
    other = 1 - idx[0] % 2
    w = 2 * NKV * D
    cols = pl.ds(al(other * w, w), w)
    send[:, :w] = q[:, cols]
    send[:, w:] = do[:, cols]


def split_q(idx, q, do, after):
    return pl.pallas_call(
        split_q_kernel,
        out_shape=jax.ShapeDtypeStruct((T, 4 * NKV * D), bf16),
        in_specs=[SM, VM, VM, ANY],
        out_specs=VM,
        compiler_params=SMALL,
        cost_estimate=cost(0.2),
        name="split_q",
    )(idx, q, do, after)


def join_q_kernel(idx, q, do, recv, qa, doa):
    a = idx[0] % 2
    w = 2 * NKV * D
    mine = pl.ds(al(a * T, T), T)
    theirs = pl.ds(al((1 - a) * T, T), T)
    cols = pl.ds(al(a * w, w), w)
    qa[mine, :] = q[:, cols]
    doa[mine, :] = do[:, cols]
    qa[theirs, :] = recv[:, :w]
    doa[theirs, :] = recv[:, w:]


def join_q(idx, q, do, recv):
    w = 2 * NKV * D
    return pl.pallas_call(
        join_q_kernel,
        out_shape=[jax.ShapeDtypeStruct((TC, w), bf16)] * 2,
        in_specs=[SM, VM, VM, VM],
        out_specs=[VM, VM],
        compiler_params=SMALL,
        cost_estimate=cost(2),
        name="join_q",
    )(idx, q, do, recv)


def unit_of(x):
    r = lax.rsqrt(jnp.mean(x * x, axis=-1, keepdims=True) + EPS)
    return x * r, r


def rows8(x, op):
    return op(x.reshape(x.shape[0] // 8, 8, x.shape[1]), axis=0)


def attn_kernel(
    n_after, idx, starts, flags, qg, kg, gains_in, q, do, kv0, kv1, kv2, *rest
):
    (
    dq, d2, d1, d0, gains,
    bias, s_scr, dp_scr, pb_scr, ds_scr, kn_scr, qn_scr, do_scr, dk_acc, dv_acc,
    ) = rest[n_after:]
    step = pl.program_id(0)
    first = (idx[0] // 2) * TC

    jl = lax.broadcasted_iota(jnp.int32, (T, T), 0)
    il = lax.broadcasted_iota(jnp.int32, (T, T), 1)
    late = jl > il

    @pl.when(step == 0)
    def _():
        gains[...] = gains_in[...]
        for qb in range(2):
            base = first + qb * T
            qpos = base + lax.broadcasted_iota(jnp.int32, (1, T), 1)
            lo = jnp.maximum(qpos - (WINDOW - 1), 0)
            for n in range(starts.shape[1]):
                b = starts[0, n]
                lo = jnp.maximum(lo, jnp.where(b <= qpos, b, 0))
            for n in range(flags.shape[1]):
                b = flags[0, n] * (n * T)
                lo = jnp.maximum(lo, jnp.where(b <= qpos, b, 0))
            for t in range(4):
                if t == 0:
                    kpos = jnp.where(late, base - WINDOW + jl, base + jl)
                else:
                    kpos = base - WINDOW + t * T + jl
                bias[qb, t] = jnp.where(kpos >= lo, 0.0, -jnp.inf).astype(f32)

    dkg = jnp.zeros((8, D), f32)
    for b, ref in enumerate((kv2, kv1, kv0)):
        xh, _ = unit_of(ref[:, :D].astype(f32))
        kn_scr[b * TC : (b + 1) * TC, :] = (xh * kg[...]).astype(bf16)
    for qb in range(2):
        for g in range(2):
            x = q[qb * T : (qb + 1) * T, g * D : (g + 1) * D].astype(f32)
            xh, _ = unit_of(x)
            qn_scr[qb, g * T : (g + 1) * T, :] = (xh * qg[...]).astype(bf16)
            do_scr[qb, g * T : (g + 1) * T, :] = do[qb * T : (qb + 1) * T, g * D : (g + 1) * D]

    def keys(kb):
        return kn_scr[kb * T : (kb + 1) * T, :]

    def vals(kb):
        ref = (kv2, kv1, kv0)[kb // 2]
        return ref[(kb % 2) * T : (kb % 2 + 1) * T, D:]

    dqg = jnp.zeros((8, D), f32)
    for qb in range(2):
        for g in range(2):
            lanes = slice(g * T, (g + 1) * T)
            qn = qn_scr[qb, lanes, :]
            dog = do_scr[qb, lanes, :]
            m = None
            for t in range(4):
                s = dot(keys(qb + t), qn, NT)
                if t == 0:
                    s = jnp.where(late, s, dot(keys(qb + 4), qn, NT))
                s = s * (SCALE * LOG2E) + bias[qb, t]
                s_scr[t] = s
                mt = rows8(s, jnp.max)
                m = mt if m is None else jnp.maximum(m, mt)
            m = jnp.max(m, axis=0, keepdims=True)
            el = None
            for t in range(4):
                e = jnp.exp2(s_scr[t] - m)
                s_scr[t] = e
                lt = rows8(e, jnp.sum)
                el = lt if el is None else el + lt
            rl = 1.0 / jnp.sum(el, axis=0, keepdims=True)
            delta = None
            for t in range(4):
                dp = dot(vals(qb + t), dog, NT)
                if t == 0:
                    dp = jnp.where(late, dp, dot(vals(qb + 4), dog, NT))
                dp_scr[t] = dp
                p = s_scr[t] * rl
                s_scr[t] = p
                pb = p.astype(bf16)
                dt = rows8(pb.astype(f32) * dp, jnp.sum)
                delta = dt if delta is None else delta + dt
                if t == 0:
                    pb_scr[0, :, lanes] = jnp.where(late, p, 0.0).astype(bf16)
                    pb_scr[4, :, lanes] = jnp.where(late, 0.0, p).astype(bf16)
                else:
                    pb_scr[t, :, lanes] = pb
            delta = jnp.sum(delta, axis=0, keepdims=True)
            for t in range(4):
                ds = s_scr[t] * (dp_scr[t] - delta) * SCALE
                if t == 0:
                    ds_scr[0, :, lanes] = jnp.where(late, ds, 0.0).astype(bf16)
                    ds_scr[4, :, lanes] = jnp.where(late, 0.0, ds).astype(bf16)
                else:
                    ds_scr[t, :, lanes] = ds.astype(bf16)
            dqn = None
            for t in range(5):
                part = dot(ds_scr[t, :, lanes], keys(qb + t), TN)
                dqn = part if dqn is None else dqn + part
            xh, r = unit_of(q[qb * T : (qb + 1) * T, g * D : (g + 1) * D].astype(f32))
            dqg = dqg + rows8(dqn * xh, jnp.sum)
            dxh = dqn * qg[...]
            dx = r * (dxh - xh * jnp.mean(dxh * xh, axis=-1, keepdims=True))
            dq[qb * T : (qb + 1) * T, g * D : (g + 1) * D] = dx.astype(bf16)
        for t in range(5):
            kb = qb + t
            rows = slice(kb * T, (kb + 1) * T)
            dv = dot(pb_scr[t], do_scr[qb], NN)
            dk = dot(ds_scr[t], qn_scr[qb], NN)
            if qb == 0 or t == 4:
                dv_acc[rows, :] = dv
                dk_acc[rows, :] = dk
            else:
                dv_acc[rows, :] += dv
                dk_acc[rows, :] += dk

    for b, (ref, out) in enumerate(((kv2, d2), (kv1, d1), (kv0, d0))):
        xh, _ = unit_of(ref[:, :D].astype(f32))
        dk = dk_acc[b * TC : (b + 1) * TC, :]
        dkg = dkg + rows8(dk * xh, jnp.sum)
        out[:, :D] = dk.astype(out.dtype)
        out[:, D:] = dv_acc[b * TC : (b + 1) * TC, :].astype(out.dtype)
    gains[0] += dqg
    gains[1] += dkg


def attn(h0, n, idx, starts, flags, qg, kg, gains, q, do, kv0, kv1, kv2, after):
    col = pl.BlockSpec((TC, 2 * D), lambda i: (0, i))
    qcol = pl.BlockSpec((TC, 2 * D), lambda i: (0, h0 + i))
    full = pl.BlockSpec((1, D), lambda i: (0, 0))
    gain = pl.BlockSpec((2, 8, D), lambda i: (0, 0, 0))
    return pl.pallas_call(
        functools.partial(attn_kernel, len(after)),
        grid=(n,),
        out_shape=[
            jax.ShapeDtypeStruct((TC, 2 * n * D), bf16),
            jax.ShapeDtypeStruct((TC, 2 * n * D), bf16),
            jax.ShapeDtypeStruct((TC, 2 * n * D), f32),
            jax.ShapeDtypeStruct((TC, 2 * n * D), f32),
            jax.ShapeDtypeStruct((2, 8, D), f32),
        ],
        in_specs=[SM, SM, SM, full, full, gain, qcol, qcol, col, col, col] + [ANY] * len(after),
        out_specs=[col, col, col, col, gain],
        scratch_shapes=[
            pltpu.VMEM((2, 4, T, T), f32),
            pltpu.VMEM((4, T, T), f32),
            pltpu.VMEM((4, T, T), f32),
            pltpu.VMEM((5, T, 2 * T), bf16),
            pltpu.VMEM((5, T, 2 * T), bf16),
            pltpu.VMEM((3 * TC, D), bf16),
            pltpu.VMEM((2, 2 * T, D), bf16),
            pltpu.VMEM((2, 2 * T, D), bf16),
            pltpu.VMEM((3 * TC, D), f32),
            pltpu.VMEM((3 * TC, D), f32),
        ],
        compiler_params=PARAMS,
        cost_estimate=cost(6 * n),
        name="attn",
    )(idx, starts, flags, qg, kg, gains, q, do, kv0, kv1, kv2, *after)


def add_kernel(x, y, *rest):
    rest[-1][...] = (x[...] + y[...].astype(f32)).astype(bf16)


def add_back(d1, r1, *after):
    return pl.pallas_call(
        add_kernel,
        out_shape=jax.ShapeDtypeStruct(r1.shape, bf16),
        in_specs=[VM, VM] + [ANY] * len(after),
        out_specs=VM,
        compiler_params=SMALL,
        cost_estimate=cost(0.2),
        name="add_back",
    )(d1, r1, *after)


def finish_kernel(n, idx, kg, d0, r2, kv, keep, send):
    a = idx[0] % 2
    for out, rows in ((keep, pl.ds(al(a * T, T), T)), (send, pl.ds(al((1 - a) * T, T), T))):
        for i in range(n):
            kc = slice(2 * i * D, (2 * i + 1) * D)
            vc = slice((2 * i + 1) * D, (2 * i + 2) * D)
            dk = d0[rows, kc] + r2[rows, kc].astype(f32)
            xh, r = unit_of(kv[rows, kc].astype(f32))
            dxh = dk * kg[...]
            dx = r * (dxh - xh * jnp.mean(dxh * xh, axis=-1, keepdims=True))
            out[:, kc] = dx.astype(bf16)
            out[:, vc] = (d0[rows, vc] + r2[rows, vc].astype(f32)).astype(bf16)


def finish(n, idx, kg, d0, r2, kv):
    return pl.pallas_call(
        functools.partial(finish_kernel, n),
        out_shape=[jax.ShapeDtypeStruct((T, 2 * n * D), bf16)] * 2,
        in_specs=[SM, VM, VM, VM, VM],
        out_specs=[VM, VM],
        compiler_params=SMALL,
        cost_estimate=cost(1),
        name="finish",
    )(idx, kg, d0, r2, kv)


def out_kv_kernel(idx, *refs):
    a = idx[0] % 2
    g = len(CHUNKS)
    keeps, recvs, (dk, dv) = refs[:g], refs[g : 2 * g], refs[2 * g :]
    h = 0
    for keep, recv, n in zip(keeps, recvs, CHUNKS):
        for i in range(n):
            for ref, side in ((keep, a), (recv, 1 - a)):
                cols = pl.ds(al(side * (NKV * D) + h * D, D), D)
                dk[:, cols] = ref[:, 2 * i * D : (2 * i + 1) * D]
                dv[:, cols] = ref[:, (2 * i + 1) * D : (2 * i + 2) * D]
            h += 1


def out_kv(idx, keeps, recvs):
    return pl.pallas_call(
        out_kv_kernel,
        out_shape=[jax.ShapeDtypeStruct((T, KEY_VALUE_HEADS * D), bf16)] * 2,
        in_specs=[SM] + [VM] * (2 * len(CHUNKS)),
        out_specs=[VM, VM],
        compiler_params=SMALL,
        cost_estimate=cost(1),
        name="out_kv",
    )(idx, *keeps, *recvs)


def split_dq_kernel(idx, *refs):
    a = idx[0] % 2
    parts, (send,) = refs[:-1], refs[-1:]
    c = 0
    for part in parts:
        w = part.shape[1]
        send[:, c : c + w] = part[pl.ds(al((1 - a) * T, T), T), :]
        c += w


def split_dq(idx, parts):
    return pl.pallas_call(
        split_dq_kernel,
        out_shape=jax.ShapeDtypeStruct((T, 2 * NKV * D), bf16),
        in_specs=[SM] + [VM] * len(parts),
        out_specs=VM,
        compiler_params=SMALL,
        cost_estimate=cost(1),
        name="split_dq",
    )(idx, *parts)


def out_q_kernel(idx, *refs):
    a = idx[0] % 2
    parts, recv, dq = refs[:-2], refs[-2], refs[-1]
    w = 2 * NKV * D
    c = 0
    for part in parts:
        n = part.shape[1]
        dq[:, pl.ds(al(a * w + c, D), n)] = part[pl.ds(al(a * T, T), T), :]
        c += n
    dq[:, pl.ds(al((1 - a) * w, w), w)] = recv[...]


def out_q(idx, parts, recv):
    return pl.pallas_call(
        out_q_kernel,
        out_shape=jax.ShapeDtypeStruct((T, QUERY_HEADS * D), bf16),
        in_specs=[SM] + [VM] * (len(parts) + 1),
        out_specs=VM,
        compiler_params=SMALL,
        cost_estimate=cost(1),
        name="out_q",
    )(idx, *parts, recv)


def along(x, distance):
    n = lax.axis_size("ctx")
    return lax.ppermute(x, "ctx", [(i, i + distance) for i in range(n) if 0 <= i + distance < n])


def swap(x, axis, bit):
    n = lax.axis_size(axis)
    return lax.ppermute(x, axis, [(i, i ^ bit) for i in range(n)])


def fold_kernel(gains, *rest):
    rest[-1][...] = jnp.sum(gains[...], axis=1)


def fold(gains, *after):
    return pl.pallas_call(
        fold_kernel,
        out_shape=jax.ShapeDtypeStruct((2, D), f32),
        in_specs=[VM] + [ANY] * len(after),
        out_specs=VM,
        compiler_params=SMALL,
        cost_estimate=cost(0.1),
        name="fold",
    )(gains, *after)


def plus_kernel(x, y, *rest):
    rest[-1][...] = x[...] + y[...]


def plus(x, y, *after):
    return pl.pallas_call(
        plus_kernel,
        out_shape=jax.ShapeDtypeStruct(x.shape, f32),
        in_specs=[VM, VM] + [ANY] * len(after),
        out_specs=VM,
        compiler_params=SMALL,
        cost_estimate=cost(0.1),
        name="plus",
    )(x, y, *after)


def on_device(q_raw, raw_keys_input, values, grad_out, q_gain, k_gain, doc_starts, flags):
    idx = lax.axis_index("ctx").astype(jnp.int32).reshape(1)
    q, k, v, do = q_raw[0], raw_keys_input[0], values[0], grad_out[0]
    qg, kg = q_gain.reshape(1, D), k_gain.reshape(1, D)
    count = len(CHUNKS)
    first = [sum(CHUNKS[:c]) for c in range(count)]

    send = split_kv(idx, k, v)
    recv = swap(send, "ctx", 1)
    kv0, kv1, kv2 = [], [], []
    for c, n in enumerate(CHUNKS):
        kv0.append(join_kv(first[c], n, idx, k, v, recv, kv1[c - 2 : c - 1] if c >= 2 else []))
        kv1.append(along(kv0[c], 2))
    kv2 = [along(x, 2) for x in kv1]
    qa, doa = join_q(idx, q, do, swap(split_q(idx, q, do, send), "ctx", 1))

    last = count - 1
    dqs, d0s, sums, r2s, gains = [], [], [], [], jnp.zeros((2, 8, D), f32)
    for c, n in enumerate(CHUNKS):
        after = kv1[c + 1 : c + 2]
        if c >= 2:
            after = after + [sums[c - 2]]
        if c >= 3:
            after = after + [r2s[c - 3]]
        dq, d2, d1, d0, gains = attn(
            first[c], n, idx, doc_starts, flags, qg, kg, gains, qa, doa, kv0[c], kv1[c], kv2[c], after
        )
        dqs.append(dq)
        d0s.append(d0)
        r1 = along(d2, -2)
        if c < last:
            sums.append(add_back(d1, r1))
            r2s.append(along(sums[c], -2))
    gain = fold(gains, sums[last - 1])
    gain = plus(gain, swap(gain, "ctx", 1))
    gain = plus(gain, swap(gain, "ctx", 2))
    sums.append(add_back(d1, r1, gain))
    r2s.append(along(sums[last], -2))
    gain = plus(gain, swap(gain, "dp", 4), sums[last], *r2s[last - 2 : last - 1])
    gain = plus(gain, swap(gain, "dp", 1), r2s[last - 1])
    gain = plus(gain, swap(gain, "dp", 2))
    gain = plus(gain, swap(gain, "ctx", 4), r2s[last])
    gain = plus(gain, swap(gain, "ctx", 16))
    gain = plus(gain, swap(gain, "ctx", 8))
    keeps, recvs = [], []
    for c, n in enumerate(CHUNKS):
        keep, send = finish(n, idx, kg, d0s[c], r2s[c], kv0[c])
        keeps.append(keep)
        recvs.append(swap(send, "ctx", 1))
    dk, dv = out_kv(idx, keeps, recvs)
    dq = out_q(idx, dqs, swap(split_dq(idx, dqs), "ctx", 1))
    return dq[None], dk[None], dv[None], gain[0], gain[1]


def solution(mesh):
    in_specs = (
        P("dp", "ctx", None),
        P("dp", "ctx", None),
        P("dp", "ctx", None),
        P("dp", "ctx", None),
        P(),
        P(),
        P("dp", None),
        P("dp", None),
    )
    out_specs = (P("dp", "ctx", None), P("dp", "ctx", None), P("dp", "ctx", None), P(), P())
    return jax.shard_map(
        on_device, mesh=mesh, in_specs=in_specs, out_specs=out_specs, check_vma=False
    )
```

```python
import functools

import jax
import jax.numpy as jnp
from jax import lax
from jax.experimental import pallas as pl
from jax.experimental.pallas import tpu as pltpu
from jax.sharding import PartitionSpec as P

QUERY_HEADS = 16
KEY_VALUE_HEADS = 8
D = 128
WINDOW = 1024
T = 256
TC = 2 * T
NKV = 4
CHUNKS = (2, 2)
LOG2E = 1.4426950408889634
SCALE = 168.0 ** (-0.5)
EPS = 1e-06

f32 = jnp.float32
bf16 = jnp.bfloat16
VM = pl.BlockSpec(memory_space=pltpu.VMEM)
ANY = pl.BlockSpec(memory_space=pl.ANY)
SM = pl.BlockSpec(memory_space=pltpu.SMEM)
PARAMS = pltpu.CompilerParams(vmem_limit_bytes=24 * 1024 * 1024)
SMALL = pltpu.CompilerParams(vmem_limit_bytes=12 * 1024 * 1024)
NT = (((1,), (1,)), ((), ()))
NN = (((1,), (0,)), ((), ()))
TN = (((0,), (0,)), ((), ()))


def dot(a, b, dims):
    return lax.dot_general(a, b, dims, preferred_element_type=f32)


def cost(us):
    return pl.CostEstimate(flops=int(us * 1e9), bytes_accessed=int(us * 1e6), transcendentals=0)


def al(x, n):
    return pl.multiple_of(x, n)


def split_kv_kernel(idx, k, v, keep, send, sems):
    a = idx[0] % 2
    copies = []
    for side, out in ((1 - a, send), (a, keep)):
        for h in range(NKV):
            cols = pl.ds(al(side * (NKV * D) + h * D, D), D)
            for x, ref in enumerate((k, v)):
                dst = out.at[:, (2 * h + x) * D : (2 * h + x + 1) * D]
                copies.append(pltpu.make_async_copy(ref.at[:, cols], dst, sems.at[len(copies)]))
    for copy in copies:
        copy.start()
    for copy in copies:
        copy.wait()


def split_kv(idx, k, v):
    return pl.pallas_call(
        split_kv_kernel,
        out_shape=[jax.ShapeDtypeStruct((T, 2 * NKV * D), bf16)] * 2,
        in_specs=[SM, ANY, ANY],
        out_specs=[VM, VM],
        scratch_shapes=[pltpu.SemaphoreType.DMA((4 * NKV,))],
        compiler_params=SMALL,
        cost_estimate=cost(1),
        name="split_kv",
    )(idx, k, v)


def join_kv_kernel(cols, idx, keep, recv, *rest):
    out = rest[-1]
    a = idx[0] % 2
    out[pl.ds(al(a * T, T), T), :] = keep[:, cols]
    out[pl.ds(al((1 - a) * T, T), T), :] = recv[:, cols]


def join_kv(h0, n, idx, keep, recv, after):
    return pl.pallas_call(
        functools.partial(join_kv_kernel, slice(2 * h0 * D, 2 * (h0 + n) * D)),
        out_shape=jax.ShapeDtypeStruct((TC, 2 * n * D), bf16),
        in_specs=[SM, VM, VM] + [ANY] * len(after),
        out_specs=VM,
        compiler_params=SMALL,
        cost_estimate=cost(0.2),
        name="join_kv",
    )(idx, keep, recv, *after)


def split_q_kernel(idx, q, do, after, send):
    other = 1 - idx[0] % 2
    w = 2 * NKV * D
    cols = pl.ds(al(other * w, w), w)
    send[:, :w] = q[:, cols]
    send[:, w:] = do[:, cols]


def split_q(idx, q, do, after):
    return pl.pallas_call(
        split_q_kernel,
        out_shape=jax.ShapeDtypeStruct((T, 4 * NKV * D), bf16),
        in_specs=[SM, VM, VM, ANY],
        out_specs=VM,
        compiler_params=SMALL,
        cost_estimate=cost(0.2),
        name="split_q",
    )(idx, q, do, after)


def join_q_kernel(idx, q, do, recv, qa, doa):
    a = idx[0] % 2
    w = 2 * NKV * D
    mine = pl.ds(al(a * T, T), T)
    theirs = pl.ds(al((1 - a) * T, T), T)
    cols = pl.ds(al(a * w, w), w)
    qa[mine, :] = q[:, cols]
    doa[mine, :] = do[:, cols]
    qa[theirs, :] = recv[:, :w]
    doa[theirs, :] = recv[:, w:]


def join_q(idx, q, do, recv):
    w = 2 * NKV * D
    return pl.pallas_call(
        join_q_kernel,
        out_shape=[jax.ShapeDtypeStruct((TC, w), bf16)] * 2,
        in_specs=[SM, VM, VM, VM],
        out_specs=[VM, VM],
        compiler_params=SMALL,
        cost_estimate=cost(2),
        name="join_q",
    )(idx, q, do, recv)


def unit_of(x):
    r = lax.rsqrt(jnp.mean(x * x, axis=-1, keepdims=True) + EPS)
    return x * r, r


def rows8(x, op):
    return op(x.reshape(x.shape[0] // 8, 8, x.shape[1]), axis=0)


def attn_kernel(
    h0, n, n_after, idx, starts, flags, qg, kg, gains_in, q, do, kv0, kv1, kv2, *rest
):
    (
    dq, d2, d1, d0, gains,
    bias, s_scr, dp_scr, pb_scr, ds_scr, kn_scr, qn_scr, do_scr, dk_acc, dv_acc,
    ) = rest[n_after:]
    first = (idx[0] // 2) * TC

    jl = lax.broadcasted_iota(jnp.int32, (T, T), 0)
    il = lax.broadcasted_iota(jnp.int32, (T, T), 1)
    late = jl > il

    if True:
        gains[...] = gains_in[...]
        for qb in range(2):
            base = first + qb * T
            qpos = base + lax.broadcasted_iota(jnp.int32, (1, T), 1)
            lo = jnp.maximum(qpos - (WINDOW - 1), 0)
            for m in range(starts.shape[1]):
                b = starts[0, m]
                lo = jnp.maximum(lo, jnp.where(b <= qpos, b, 0))
            for m in range(flags.shape[1]):
                b = flags[0, m] * (m * T)
                lo = jnp.maximum(lo, jnp.where(b <= qpos, b, 0))
            for t in range(4):
                if t == 0:
                    kpos = jnp.where(late, base - WINDOW + jl, base + jl)
                else:
                    kpos = base - WINDOW + t * T + jl
                bias[qb, t] = jnp.where(kpos >= lo, 0.0, -jnp.inf).astype(f32)

    for h in range(n):
        kc = slice(2 * h * D, (2 * h + 1) * D)
        vc = slice((2 * h + 1) * D, (2 * h + 2) * D)
        R = 128
        for b, ref in enumerate((kv2, kv1, kv0)):
            xh, _ = unit_of(ref[:, kc].astype(f32))
            kn_scr[b * TC : (b + 1) * TC, :] = (xh * kg[...]).astype(bf16)
        for qb in range(2):
            for g in range(2):
                rows = slice((2 * qb + g) * T, (2 * qb + g + 1) * T)
                xh, _ = unit_of(q[qb * T : (qb + 1) * T, (2 * (h0 + h) + g) * D : (2 * (h0 + h) + g + 1) * D].astype(f32))
                qn_scr[rows, :] = (xh * qg[...]).astype(bf16)
                do_scr[rows, :] = do[qb * T : (qb + 1) * T, (2 * (h0 + h) + g) * D : (2 * (h0 + h) + g + 1) * D]

        kvs = (kv2, kv1, kv0)

        def vals(row):
            return kvs[row // TC][row % TC : row % TC + R, vc]

        def late_of(r):
            return jl[:R] + r * R > il[:R]

        tasks = [(t, r) for t in range(4) for r in range(T // R)]
        st = [dict(m=None, l=None, delta=None) for _ in range(4)]

        def span(i):
            return slice(i * T, (i + 1) * T)

        def join(x, y, op):
            return y if x is None else op(x, y)

        def scores(i, t, r):
            qb, row = i // 2, (i // 2 + t) * T + r * R
            s = dot(kn_scr[row : row + R, :], qn_scr[span(i), :], NT)
            if t == 0:
                far = dot(kn_scr[row + 4 * T : row + 4 * T + R, :], qn_scr[span(i), :], NT)
                s = jnp.where(late_of(r), s, far)
            s = s * (SCALE * LOG2E) + bias[qb, t, r * R : (r + 1) * R, :]
            s_scr[i % 2, t * T + r * R : t * T + (r + 1) * R, :] = s
            st[i]["m"] = join(st[i]["m"], rows8(s, jnp.max), jnp.maximum)

        def grads(i, t, r):
            row = (i // 2 + t) * T + r * R
            dp = dot(vals(row), do_scr[span(i), :], NT)
            if t == 0:
                dp = jnp.where(late_of(r), dp, dot(vals(row + 4 * T), do_scr[span(i), :], NT))
            dp_scr[i % 2, t * T + r * R : t * T + (r + 1) * R, :] = dp

        def expo(i, t, r):
            rows = slice(t * T + r * R, t * T + (r + 1) * R)
            e = jnp.exp2(s_scr[i % 2, rows, :] - st[i]["m"])
            s_scr[i % 2, rows, :] = e
            st[i]["l"] = join(st[i]["l"], rows8(e, jnp.sum), jnp.add)

        def store(ref, i, t, r, x):
            row = (i // 2 + t) * T + r * R
            if t == 0:
                late = late_of(r)
                ref[row : row + R, span(i)] = jnp.where(late, x, 0.0).astype(bf16)
                ref[row + 4 * T : row + 4 * T + R, span(i)] = jnp.where(late, 0.0, x).astype(bf16)
            else:
                ref[row : row + R, span(i)] = x.astype(bf16)

        def probs(i, t, r):
            rows = slice(t * T + r * R, t * T + (r + 1) * R)
            p = s_scr[i % 2, rows, :] * st[i]["rl"]
            store(pb_scr, i, t, r, p)
            d = rows8(p.astype(bf16).astype(f32) * dp_scr[i % 2, rows, :], jnp.sum)
            st[i]["delta"] = join(st[i]["delta"], d, jnp.add)

        def dscores(i, t, r):
            rows = slice(t * T + r * R, t * T + (r + 1) * R)
            ds = s_scr[i % 2, rows, :] * (dp_scr[i % 2, rows, :] - st[i]["delta"]) * st[i]["rs"]
            store(ds_scr, i, t, r, ds)

        dqg = []

        def dquery(i):
            qb, g = i // 2, i % 2
            rows, cols = slice(qb * T, (qb + 1) * T), slice((2 * h + g) * D, (2 * h + g + 1) * D)
            dqn = dot(ds_scr[qb * T : (qb + 5) * T, span(i)], kn_scr[qb * T : (qb + 5) * T, :], TN)
            xh, r = unit_of(q[rows, slice((2 * (h0 + h) + g) * D, (2 * (h0 + h) + g + 1) * D)].astype(f32))
            dqg.append(rows8(dqn * xh, jnp.sum))
            dxh = dqn * qg[...]
            dx = r * (dxh - xh * jnp.mean(dxh * xh, axis=-1, keepdims=True))
            dq[rows, cols] = dx.astype(bf16)

        def do_all(fs):
            for tr in tasks:
                for f in fs:
                    f(*tr)

        def top(f, i):
            return lambda t, r: f(i, t, r)

        def dkeys(k0, k1, l0, l1):
            rows, lanes = slice(k0 * T, k1 * T), slice(l0 * T, l1 * T)
            dv_acc[rows, :] = dot(pb_scr[rows, lanes], do_scr[lanes, :], NN)
            dk_acc[rows, :] = dot(ds_scr[rows, lanes], qn_scr[lanes, :], NN)

        inter = False
        do_all([top(scores, 0)])
        for i in range(4):
            st[i]["m"] = jnp.max(st[i]["m"], axis=0, keepdims=True)
            do_all([top(expo, i), top(grads, i)])
            st[i]["rl"] = 1.0 / jnp.sum(st[i]["l"], axis=0, keepdims=True)
            st[i]["rs"] = st[i]["rl"] * SCALE
            do_all([top(probs, i)] + ([top(scores, i + 1)] if inter and i < 3 else []))
            st[i]["delta"] = jnp.sum(st[i]["delta"], axis=0, keepdims=True)
            if inter and i > 0:
                dquery(i - 1)
            do_all([top(dscores, i)] + ([top(scores, i + 1)] if not inter and i < 3 else []))
            if not inter:
                dquery(i)
        if inter:
            dquery(3)
        dkeys(0, 1, 0, 2)
        for kb in range(1, 5):
            dkeys(kb, kb + 1, 0, 4)
        dkeys(5, 6, 2, 4)

        dkg = jnp.zeros((8, D), f32)
        for b, (ref, out) in enumerate(((kv2, d2), (kv1, d1), (kv0, d0))):
            xh, _ = unit_of(ref[:, kc].astype(f32))
            dk = dk_acc[b * TC : (b + 1) * TC, :]
            dkg = dkg + rows8(dk * xh, jnp.sum)
            out[:, kc] = dk.astype(out.dtype)
            out[:, vc] = dv_acc[b * TC : (b + 1) * TC, :].astype(out.dtype)
        gains[0] += dqg[0] + dqg[1] + dqg[2] + dqg[3]
        gains[1] += dkg


def attn(h0, n, idx, starts, flags, qg, kg, gains, q, do, kv0, kv1, kv2, after):
    return pl.pallas_call(
        functools.partial(attn_kernel, h0, n, len(after)),
        out_shape=[
            jax.ShapeDtypeStruct((TC, 2 * n * D), bf16),
            jax.ShapeDtypeStruct((TC, 2 * n * D), bf16),
            jax.ShapeDtypeStruct((TC, 2 * n * D), f32),
            jax.ShapeDtypeStruct((TC, 2 * n * D), f32),
            jax.ShapeDtypeStruct((2, 8, D), f32),
        ],
        in_specs=[SM] * 3 + [VM] * 8 + [ANY] * len(after),
        out_specs=[VM] * 5,
        scratch_shapes=[
            pltpu.VMEM((2, 4, T, T), f32),
            pltpu.VMEM((2, WINDOW, T), f32),
            pltpu.VMEM((2, WINDOW, T), f32),
            pltpu.VMEM((3 * TC, 4 * T), bf16),
            pltpu.VMEM((3 * TC, 4 * T), bf16),
            pltpu.VMEM((3 * TC, D), bf16),
            pltpu.VMEM((4 * T, D), bf16),
            pltpu.VMEM((4 * T, D), bf16),
            pltpu.VMEM((3 * TC, D), f32),
            pltpu.VMEM((3 * TC, D), f32),
        ],
        compiler_params=PARAMS,
        cost_estimate=cost(6 * n),
        name="attn",
    )(idx, starts, flags, qg, kg, gains, q, do, kv0, kv1, kv2, *after)


def add_kernel(x, y, *rest):
    rest[-1][...] = (x[...] + y[...].astype(f32)).astype(bf16)


def add_back(d1, r1, *after):
    return pl.pallas_call(
        add_kernel,
        out_shape=jax.ShapeDtypeStruct(r1.shape, bf16),
        in_specs=[VM, VM] + [ANY] * len(after),
        out_specs=VM,
        compiler_params=SMALL,
        cost_estimate=cost(0.2),
        name="add_back",
    )(d1, r1, *after)


def finish_kernel(n, idx, kg, d0, r2, kv, keep, send):
    a = idx[0] % 2
    for out, rows in ((keep, pl.ds(al(a * T, T), T)), (send, pl.ds(al((1 - a) * T, T), T))):
        for i in range(n):
            kc = slice(2 * i * D, (2 * i + 1) * D)
            vc = slice((2 * i + 1) * D, (2 * i + 2) * D)
            dk = d0[rows, kc] + r2[rows, kc].astype(f32)
            xh, r = unit_of(kv[rows, kc].astype(f32))
            dxh = dk * kg[...]
            dx = r * (dxh - xh * jnp.mean(dxh * xh, axis=-1, keepdims=True))
            out[:, kc] = dx.astype(bf16)
            out[:, vc] = (d0[rows, vc] + r2[rows, vc].astype(f32)).astype(bf16)


def finish(n, idx, kg, d0, r2, kv):
    return pl.pallas_call(
        functools.partial(finish_kernel, n),
        out_shape=[jax.ShapeDtypeStruct((T, 2 * n * D), bf16)] * 2,
        in_specs=[SM, VM, VM, VM, VM],
        out_specs=[VM, VM],
        compiler_params=SMALL,
        cost_estimate=cost(1),
        name="finish",
    )(idx, kg, d0, r2, kv)


def out_kv_kernel(idx, *refs):
    a = idx[0] % 2
    g = len(CHUNKS)
    keeps, recvs, (dk, dv) = refs[:g], refs[g : 2 * g], refs[2 * g :]
    h = 0
    for keep, recv, n in zip(keeps, recvs, CHUNKS):
        for i in range(n):
            for ref, side in ((keep, a), (recv, 1 - a)):
                cols = pl.ds(al(side * (NKV * D) + h * D, D), D)
                dk[:, cols] = ref[:, 2 * i * D : (2 * i + 1) * D]
                dv[:, cols] = ref[:, (2 * i + 1) * D : (2 * i + 2) * D]
            h += 1


def out_kv(idx, keeps, recvs):
    return pl.pallas_call(
        out_kv_kernel,
        out_shape=[jax.ShapeDtypeStruct((T, KEY_VALUE_HEADS * D), bf16)] * 2,
        in_specs=[SM] + [VM] * (2 * len(CHUNKS)),
        out_specs=[VM, VM],
        compiler_params=SMALL,
        cost_estimate=cost(1),
        name="out_kv",
    )(idx, *keeps, *recvs)


def split_dq_kernel(idx, *refs):
    a = idx[0] % 2
    parts, (send,) = refs[:-1], refs[-1:]
    c = 0
    for part in parts:
        w = part.shape[1]
        send[:, c : c + w] = part[pl.ds(al((1 - a) * T, T), T), :]
        c += w


def split_dq(idx, parts):
    return pl.pallas_call(
        split_dq_kernel,
        out_shape=jax.ShapeDtypeStruct((T, 2 * NKV * D), bf16),
        in_specs=[SM] + [VM] * len(parts),
        out_specs=VM,
        compiler_params=SMALL,
        cost_estimate=cost(1),
        name="split_dq",
    )(idx, *parts)


def out_q_kernel(idx, *refs):
    a = idx[0] % 2
    parts, recv, dq = refs[:-2], refs[-2], refs[-1]
    w = 2 * NKV * D
    c = 0
    for part in parts:
        n = part.shape[1]
        dq[:, pl.ds(al(a * w + c, D), n)] = part[pl.ds(al(a * T, T), T), :]
        c += n
    dq[:, pl.ds(al((1 - a) * w, w), w)] = recv[...]


def out_q(idx, parts, recv):
    return pl.pallas_call(
        out_q_kernel,
        out_shape=jax.ShapeDtypeStruct((T, QUERY_HEADS * D), bf16),
        in_specs=[SM] + [VM] * (len(parts) + 1),
        out_specs=VM,
        compiler_params=SMALL,
        cost_estimate=cost(1),
        name="out_q",
    )(idx, *parts, recv)


def along(x, distance):
    n = lax.axis_size("ctx")
    return lax.ppermute(x, "ctx", [(i, i + distance) for i in range(n) if 0 <= i + distance < n])


def swap(x, axis, bit):
    n = lax.axis_size(axis)
    return lax.ppermute(x, axis, [(i, i ^ bit) for i in range(n)])


def fold_kernel(gains, *rest):
    rest[-1][...] = jnp.sum(gains[...], axis=1)


def fold(gains, *after):
    return pl.pallas_call(
        fold_kernel,
        out_shape=jax.ShapeDtypeStruct((2, D), f32),
        in_specs=[VM] + [ANY] * len(after),
        out_specs=VM,
        compiler_params=SMALL,
        cost_estimate=cost(0.1),
        name="fold",
    )(gains, *after)


def plus_kernel(x, y, *rest):
    rest[-1][...] = x[...] + y[...]


def plus(x, y, *after):
    return pl.pallas_call(
        plus_kernel,
        out_shape=jax.ShapeDtypeStruct(x.shape, f32),
        in_specs=[VM, VM] + [ANY] * len(after),
        out_specs=VM,
        compiler_params=SMALL,
        cost_estimate=cost(0.1),
        name="plus",
    )(x, y, *after)


def on_device(q_raw, raw_keys_input, values, grad_out, q_gain, k_gain, doc_starts, flags):
    idx = lax.axis_index("ctx").astype(jnp.int32).reshape(1)
    q, k, v, do = q_raw[0], raw_keys_input[0], values[0], grad_out[0]
    qg, kg = q_gain.reshape(1, D), k_gain.reshape(1, D)
    count = len(CHUNKS)
    first = [sum(CHUNKS[:c]) for c in range(count)]

    keep, send = split_kv(idx, k, v)
    recv = swap(send, "ctx", 1)
    kv0, kv1, kv2 = [], [], []
    for c, n in enumerate(CHUNKS):
        kv0.append(join_kv(first[c], n, idx, keep, recv, kv1[c - 1 : c] if c >= 2 else []))
        kv1.append(along(kv0[c], 2))
    kv2 = [along(x, 2) for x in kv1]
    qa, doa = join_q(idx, q, do, swap(split_q(idx, q, do, kv0[0]), "ctx", 1))

    last = count - 1
    dqs, d0s, sums, r2s, gains = [], [], [], [], jnp.zeros((2, 8, D), f32)
    for c, n in enumerate(CHUNKS):
        after = kv1[c + 1 : c + 2]
        if c >= 2:
            after = after + [sums[c - 2]]
        if c >= 3:
            after = after + [r2s[c - 3]]
        dq, d2, d1, d0, gains = attn(
            first[c], n, idx, doc_starts, flags, qg, kg, gains, qa, doa, kv0[c], kv1[c], kv2[c], after
        )
        dqs.append(dq)
        d0s.append(d0)
        r1 = along(d2, -2)
        if c < last:
            sums.append(add_back(d1, r1))
            r2s.append(along(sums[c], -2))
    gain = fold(gains, sums[last - 1])
    gain = plus(gain, swap(gain, "ctx", 1))
    gain = plus(gain, swap(gain, "dp", 1))
    gain = plus(gain, swap(gain, "dp", 2))
    sums.append(add_back(d1, r1, gain))
    r2s.append(along(sums[last], -2))
    gain = plus(gain, swap(gain, "dp", 4), sums[last], *r2s[last - 2 : last - 1])
    gain = plus(gain, swap(gain, "ctx", 16), r2s[last - 1])
    gain = plus(gain, swap(gain, "ctx", 2), r2s[last])
    gain = plus(gain, swap(gain, "ctx", 4))
    gain = plus(gain, swap(gain, "ctx", 8))
    keeps, recvs = [], []
    for c, n in enumerate(CHUNKS):
        keep, send = finish(n, idx, kg, d0s[c], r2s[c], kv0[c])
        keeps.append(keep)
        recvs.append(swap(send, "ctx", 1))
    dk, dv = out_kv(idx, keeps, recvs)
    dq = out_q(idx, dqs, swap(split_dq(idx, dqs), "ctx", 1))
    return dq[None], dk[None], dv[None], gain[0], gain[1]


def solution(mesh):
    in_specs = (
        P("dp", "ctx", None),
        P("dp", "ctx", None),
        P("dp", "ctx", None),
        P("dp", "ctx", None),
        P(),
        P(),
        P("dp", None),
        P("dp", None),
    )
    out_specs = (P("dp", "ctx", None), P("dp", "ctx", None), P("dp", "ctx", None), P(), P())
    return jax.shard_map(
        on_device, mesh=mesh, in_specs=in_specs, out_specs=out_specs, check_vma=False
    )
```

```python
import functools

import jax
import jax.numpy as jnp
from jax import lax
from jax.experimental import pallas as pl
from jax.experimental.pallas import tpu as pltpu
from jax.sharding import PartitionSpec as P

QUERY_HEADS = 16
KEY_VALUE_HEADS = 8
D = 128
WINDOW = 1024
T = 256
TC = 2 * T
NKV = 4
CHUNKS = (2, 2)
LOG2E = 1.4426950408889634
SCALE = 168.0 ** (-0.5)
EPS = 1e-06

f32 = jnp.float32
bf16 = jnp.bfloat16
VM = pl.BlockSpec(memory_space=pltpu.VMEM)
ANY = pl.BlockSpec(memory_space=pl.ANY)
SM = pl.BlockSpec(memory_space=pltpu.SMEM)
PARAMS = pltpu.CompilerParams(vmem_limit_bytes=24 * 1024 * 1024)
SMALL = pltpu.CompilerParams(vmem_limit_bytes=12 * 1024 * 1024)
NT = (((1,), (1,)), ((), ()))
NN = (((1,), (0,)), ((), ()))
TN = (((0,), (0,)), ((), ()))


def dot(a, b, dims):
    return lax.dot_general(a, b, dims, preferred_element_type=f32)


def cost(us):
    return pl.CostEstimate(flops=int(us * 1e9), bytes_accessed=int(us * 1e6), transcendentals=0)


def al(x, n):
    return pl.multiple_of(x, n)


def split_kv_kernel(idx, k, v, keep, send, sems):
    a = idx[0] % 2
    copies = []
    for side, out in ((1 - a, send), (a, keep)):
        for h in range(NKV):
            cols = pl.ds(al(side * (NKV * D) + h * D, D), D)
            for x, ref in enumerate((k, v)):
                dst = out.at[:, (2 * h + x) * D : (2 * h + x + 1) * D]
                copies.append(pltpu.make_async_copy(ref.at[:, cols], dst, sems.at[len(copies)]))
    for copy in copies:
        copy.start()
    for copy in copies:
        copy.wait()


def split_kv(idx, k, v):
    return pl.pallas_call(
        split_kv_kernel,
        out_shape=[jax.ShapeDtypeStruct((T, 2 * NKV * D), bf16)] * 2,
        in_specs=[SM, ANY, ANY],
        out_specs=[VM, VM],
        scratch_shapes=[pltpu.SemaphoreType.DMA((4 * NKV,))],
        compiler_params=SMALL,
        cost_estimate=cost(1),
        name="split_kv",
    )(idx, k, v)


def join_kv_kernel(cols, idx, keep, recv, *rest):
    out = rest[-1]
    a = idx[0] % 2
    out[pl.ds(al(a * T, T), T), :] = keep[:, cols]
    out[pl.ds(al((1 - a) * T, T), T), :] = recv[:, cols]


def join_kv(h0, n, idx, keep, recv, after):
    return pl.pallas_call(
        functools.partial(join_kv_kernel, slice(2 * h0 * D, 2 * (h0 + n) * D)),
        out_shape=jax.ShapeDtypeStruct((TC, 2 * n * D), bf16),
        in_specs=[SM, VM, VM] + [ANY] * len(after),
        out_specs=VM,
        compiler_params=SMALL,
        cost_estimate=cost(0.2),
        name="join_kv",
    )(idx, keep, recv, *after)


def split_q_kernel(idx, q, do, after, send):
    other = 1 - idx[0] % 2
    w = 2 * NKV * D
    cols = pl.ds(al(other * w, w), w)
    send[:, :w] = q[:, cols]
    send[:, w:] = do[:, cols]


def split_q(idx, q, do, after):
    return pl.pallas_call(
        split_q_kernel,
        out_shape=jax.ShapeDtypeStruct((T, 4 * NKV * D), bf16),
        in_specs=[SM, VM, VM, ANY],
        out_specs=VM,
        compiler_params=SMALL,
        cost_estimate=cost(0.2),
        name="split_q",
    )(idx, q, do, after)


def join_q_kernel(idx, q, do, recv, qa, doa):
    a = idx[0] % 2
    w = 2 * NKV * D
    mine = pl.ds(al(a * T, T), T)
    theirs = pl.ds(al((1 - a) * T, T), T)
    cols = pl.ds(al(a * w, w), w)
    qa[mine, :] = q[:, cols]
    doa[mine, :] = do[:, cols]
    qa[theirs, :] = recv[:, :w]
    doa[theirs, :] = recv[:, w:]


def join_q(idx, q, do, recv):
    w = 2 * NKV * D
    return pl.pallas_call(
        join_q_kernel,
        out_shape=[jax.ShapeDtypeStruct((TC, w), bf16)] * 2,
        in_specs=[SM, VM, VM, VM],
        out_specs=[VM, VM],
        compiler_params=SMALL,
        cost_estimate=cost(2),
        name="join_q",
    )(idx, q, do, recv)


def unit_of(x):
    r = lax.rsqrt(jnp.mean(x * x, axis=-1, keepdims=True) + EPS)
    return x * r, r


def rows8(x, op):
    return op(x.reshape(x.shape[0] // 8, 8, x.shape[1]), axis=0)


def attn_kernel(
    h0, n, n_after, idx, starts, flags, qg, kg, gains_in, q, do, kv0, kv1, kv2, *rest
):
    (
    dq, d2, d1, d0, gains,
    bias, s_scr, dp_scr, pb_scr, ds_scr, kn_scr, qn_scr, do_scr, dk_acc, dv_acc,
    ) = rest[n_after:]
    first = (idx[0] // 2) * TC

    jl = lax.broadcasted_iota(jnp.int32, (T, T), 0)
    il = lax.broadcasted_iota(jnp.int32, (T, T), 1)
    late = jl > il

    if True:
        gains[...] = gains_in[...]
        for qb in range(2):
            base = first + qb * T
            qpos = base + lax.broadcasted_iota(jnp.int32, (1, T), 1)
            lo = jnp.maximum(qpos - (WINDOW - 1), 0)
            for m in range(starts.shape[1]):
                b = starts[0, m]
                lo = jnp.maximum(lo, jnp.where(b <= qpos, b, 0))
            for m in range(flags.shape[1]):
                b = flags[0, m] * (m * T)
                lo = jnp.maximum(lo, jnp.where(b <= qpos, b, 0))
            for t in range(4):
                if t == 0:
                    kpos = jnp.where(late, base - WINDOW + jl, base + jl)
                else:
                    kpos = base - WINDOW + t * T + jl
                bias[qb, t] = jnp.where(kpos >= lo, 0.0, -jnp.inf).astype(f32)

    for h in range(n):
        kc = slice(2 * h * D, (2 * h + 1) * D)
        vc = slice((2 * h + 1) * D, (2 * h + 2) * D)
        R = 128
        for b, ref in enumerate((kv2, kv1, kv0)):
            xh, _ = unit_of(ref[:, kc].astype(f32))
            kn_scr[b * TC : (b + 1) * TC, :] = (xh * kg[...]).astype(bf16)
        for qb in range(2):
            for g in range(2):
                rows = slice((2 * qb + g) * T, (2 * qb + g + 1) * T)
                xh, _ = unit_of(q[qb * T : (qb + 1) * T, (2 * (h0 + h) + g) * D : (2 * (h0 + h) + g + 1) * D].astype(f32))
                qn_scr[rows, :] = (xh * qg[...]).astype(bf16)
                do_scr[rows, :] = do[qb * T : (qb + 1) * T, (2 * (h0 + h) + g) * D : (2 * (h0 + h) + g + 1) * D]

        kvs = (kv2, kv1, kv0)

        def vals(row):
            return kvs[row // TC][row % TC : row % TC + R, vc]

        def late_of(r):
            return jl[:R] + r * R > il[:R]

        tasks = [(t, r) for t in range(4) for r in range(T // R)]
        st = [dict(m=None, l=None, delta=None) for _ in range(4)]

        def span(i):
            return slice(i * T, (i + 1) * T)

        def join(x, y, op):
            return y if x is None else op(x, y)

        def scores(i, t, r):
            qb, row = i // 2, (i // 2 + t) * T + r * R
            s = dot(kn_scr[row : row + R, :], qn_scr[span(i), :], NT)
            if t == 0:
                far = dot(kn_scr[row + 4 * T : row + 4 * T + R, :], qn_scr[span(i), :], NT)
                s = jnp.where(late_of(r), s, far)
            s = s * (SCALE * LOG2E) + bias[qb, t, r * R : (r + 1) * R, :]
            s_scr[i % 2, t * T + r * R : t * T + (r + 1) * R, :] = s
            st[i]["m"] = join(st[i]["m"], rows8(s, jnp.max), jnp.maximum)

        def grads(i, t, r):
            row = (i // 2 + t) * T + r * R
            dp = dot(vals(row), do_scr[span(i), :], NT)
            if t == 0:
                dp = jnp.where(late_of(r), dp, dot(vals(row + 4 * T), do_scr[span(i), :], NT))
            dp_scr[i % 2, t * T + r * R : t * T + (r + 1) * R, :] = dp

        def expo(i, t, r):
            rows = slice(t * T + r * R, t * T + (r + 1) * R)
            e = jnp.exp2(s_scr[i % 2, rows, :] - st[i]["m"])
            s_scr[i % 2, rows, :] = e
            st[i]["l"] = join(st[i]["l"], rows8(e, jnp.sum), jnp.add)

        def store(ref, i, t, r, x):
            row = (i // 2 + t) * T + r * R
            if t == 0:
                late = late_of(r)
                ref[row : row + R, span(i)] = jnp.where(late, x, 0.0).astype(bf16)
                ref[row + 4 * T : row + 4 * T + R, span(i)] = jnp.where(late, 0.0, x).astype(bf16)
            else:
                ref[row : row + R, span(i)] = x.astype(bf16)

        def probs(i, t, r):
            rows = slice(t * T + r * R, t * T + (r + 1) * R)
            p = s_scr[i % 2, rows, :] * st[i]["rl"]
            store(pb_scr, i, t, r, p)
            d = rows8(p.astype(bf16).astype(f32) * dp_scr[i % 2, rows, :], jnp.sum)
            st[i]["delta"] = join(st[i]["delta"], d, jnp.add)

        def dscores(i, t, r):
            rows = slice(t * T + r * R, t * T + (r + 1) * R)
            ds = s_scr[i % 2, rows, :] * (dp_scr[i % 2, rows, :] - st[i]["delta"]) * st[i]["rs"]
            store(ds_scr, i, t, r, ds)

        dqg = []

        def dquery(i):
            qb, g = i // 2, i % 2
            rows, cols = slice(qb * T, (qb + 1) * T), slice((2 * h + g) * D, (2 * h + g + 1) * D)
            dqn = dot(ds_scr[qb * T : (qb + 5) * T, span(i)], kn_scr[qb * T : (qb + 5) * T, :], TN)
            xh, r = unit_of(q[rows, slice((2 * (h0 + h) + g) * D, (2 * (h0 + h) + g + 1) * D)].astype(f32))
            dqg.append(rows8(dqn * xh, jnp.sum))
            dxh = dqn * qg[...]
            dx = r * (dxh - xh * jnp.mean(dxh * xh, axis=-1, keepdims=True))
            dq[rows, cols] = dx.astype(bf16)

        def do_all(fs):
            for tr in tasks:
                for f in fs:
                    f(*tr)

        def top(f, i):
            return lambda t, r: f(i, t, r)

        def dkeys(k0, k1, l0, l1):
            rows, lanes = slice(k0 * T, k1 * T), slice(l0 * T, l1 * T)
            dv_acc[rows, :] = dot(pb_scr[rows, lanes], do_scr[lanes, :], NN)
            dk_acc[rows, :] = dot(ds_scr[rows, lanes], qn_scr[lanes, :], NN)

        inter = False
        do_all([top(scores, 0)])
        for i in range(4):
            st[i]["m"] = jnp.max(st[i]["m"], axis=0, keepdims=True)
            do_all([top(expo, i), top(grads, i)])
            st[i]["rl"] = 1.0 / jnp.sum(st[i]["l"], axis=0, keepdims=True)
            st[i]["rs"] = st[i]["rl"] * SCALE
            do_all([top(probs, i)] + ([top(scores, i + 1)] if inter and i < 3 else []))
            st[i]["delta"] = jnp.sum(st[i]["delta"], axis=0, keepdims=True)
            if inter and i > 0:
                dquery(i - 1)
            do_all([top(dscores, i)] + ([top(scores, i + 1)] if not inter and i < 3 else []))
            if not inter:
                dquery(i)
        if inter:
            dquery(3)
        dkeys(0, 1, 0, 2)
        for kb in range(1, 5):
            dkeys(kb, kb + 1, 0, 4)
        dkeys(5, 6, 2, 4)

        dkg = jnp.zeros((8, D), f32)
        for b, (ref, out) in enumerate(((kv2, d2), (kv1, d1), (kv0, d0))):
            xh, _ = unit_of(ref[:, kc].astype(f32))
            dk = dk_acc[b * TC : (b + 1) * TC, :]
            dkg = dkg + rows8(dk * xh, jnp.sum)
            out[:, kc] = dk.astype(out.dtype)
            out[:, vc] = dv_acc[b * TC : (b + 1) * TC, :].astype(out.dtype)
        gains[0] += dqg[0] + dqg[1] + dqg[2] + dqg[3]
        gains[1] += dkg


def attn(h0, n, idx, starts, flags, qg, kg, gains, q, do, kv0, kv1, kv2, after):
    return pl.pallas_call(
        functools.partial(attn_kernel, h0, n, len(after)),
        out_shape=[
            jax.ShapeDtypeStruct((TC, 2 * n * D), bf16),
            jax.ShapeDtypeStruct((TC, 2 * n * D), bf16),
            jax.ShapeDtypeStruct((TC, 2 * n * D), f32),
            jax.ShapeDtypeStruct((TC, 2 * n * D), f32),
            jax.ShapeDtypeStruct((2, 8, D), f32),
        ],
        in_specs=[SM] * 3 + [VM] * 8 + [ANY] * len(after),
        out_specs=[VM] * 5,
        scratch_shapes=[
            pltpu.VMEM((2, 4, T, T), f32),
            pltpu.VMEM((2, WINDOW, T), f32),
            pltpu.VMEM((2, WINDOW, T), f32),
            pltpu.VMEM((3 * TC, 4 * T), bf16),
            pltpu.VMEM((3 * TC, 4 * T), bf16),
            pltpu.VMEM((3 * TC, D), bf16),
            pltpu.VMEM((4 * T, D), bf16),
            pltpu.VMEM((4 * T, D), bf16),
            pltpu.VMEM((3 * TC, D), f32),
            pltpu.VMEM((3 * TC, D), f32),
        ],
        compiler_params=PARAMS,
        cost_estimate=cost(6 * n),
        name="attn",
    )(idx, starts, flags, qg, kg, gains, q, do, kv0, kv1, kv2, *after)


def add_kernel(x, y, *rest):
    rest[-1][...] = (x[...] + y[...].astype(f32)).astype(bf16)


def add_back(d1, r1, *after):
    return pl.pallas_call(
        add_kernel,
        out_shape=jax.ShapeDtypeStruct(r1.shape, bf16),
        in_specs=[VM, VM] + [ANY] * len(after),
        out_specs=VM,
        compiler_params=SMALL,
        cost_estimate=cost(0.2),
        name="add_back",
    )(d1, r1, *after)


def finish_kernel(n, idx, kg, d0, r2, kv, after, keep, send):
    a = idx[0] % 2
    for out, rows in ((keep, pl.ds(al(a * T, T), T)), (send, pl.ds(al((1 - a) * T, T), T))):
        for i in range(n):
            kc = slice(2 * i * D, (2 * i + 1) * D)
            vc = slice((2 * i + 1) * D, (2 * i + 2) * D)
            dk = d0[rows, kc] + r2[rows, kc].astype(f32)
            xh, r = unit_of(kv[rows, kc].astype(f32))
            dxh = dk * kg[...]
            dx = r * (dxh - xh * jnp.mean(dxh * xh, axis=-1, keepdims=True))
            out[:, kc] = dx.astype(bf16)
            out[:, vc] = (d0[rows, vc] + r2[rows, vc].astype(f32)).astype(bf16)


def finish(n, idx, kg, d0, r2, kv, after):
    return pl.pallas_call(
        functools.partial(finish_kernel, n),
        out_shape=[jax.ShapeDtypeStruct((T, 2 * n * D), bf16)] * 2,
        in_specs=[SM, VM, VM, VM, VM, ANY],
        out_specs=[VM, VM],
        compiler_params=SMALL,
        cost_estimate=cost(1),
        name="finish",
    )(idx, kg, d0, r2, kv, after)


def out_kv_kernel(idx, *refs):
    a = idx[0] % 2
    g = len(CHUNKS)
    keeps, recvs, (dk, dv) = refs[:g], refs[g : 2 * g], refs[2 * g :]
    h = 0
    for keep, recv, n in zip(keeps, recvs, CHUNKS):
        for i in range(n):
            for ref, side in ((keep, a), (recv, 1 - a)):
                cols = pl.ds(al(side * (NKV * D) + h * D, D), D)
                dk[:, cols] = ref[:, 2 * i * D : (2 * i + 1) * D]
                dv[:, cols] = ref[:, (2 * i + 1) * D : (2 * i + 2) * D]
            h += 1


def out_kv(idx, keeps, recvs):
    return pl.pallas_call(
        out_kv_kernel,
        out_shape=[jax.ShapeDtypeStruct((T, KEY_VALUE_HEADS * D), bf16)] * 2,
        in_specs=[SM] + [VM] * (2 * len(CHUNKS)),
        out_specs=[VM, VM],
        compiler_params=SMALL,
        cost_estimate=cost(1),
        name="out_kv",
    )(idx, *keeps, *recvs)


def split_dq_kernel(idx, *refs):
    a = idx[0] % 2
    parts, (send,) = refs[:-1], refs[-1:]
    c = 0
    for part in parts:
        w = part.shape[1]
        send[:, c : c + w] = part[pl.ds(al((1 - a) * T, T), T), :]
        c += w


def split_dq(idx, parts):
    return pl.pallas_call(
        split_dq_kernel,
        out_shape=jax.ShapeDtypeStruct((T, 2 * NKV * D), bf16),
        in_specs=[SM] + [VM] * len(parts),
        out_specs=VM,
        compiler_params=SMALL,
        cost_estimate=cost(1),
        name="split_dq",
    )(idx, *parts)


def out_q_kernel(idx, *refs):
    a = idx[0] % 2
    parts, recv, dq = refs[:-2], refs[-2], refs[-1]
    w = 2 * NKV * D
    c = 0
    for part in parts:
        n = part.shape[1]
        dq[:, pl.ds(al(a * w + c, D), n)] = part[pl.ds(al(a * T, T), T), :]
        c += n
    dq[:, pl.ds(al((1 - a) * w, w), w)] = recv[...]


def out_q(idx, parts, recv):
    return pl.pallas_call(
        out_q_kernel,
        out_shape=jax.ShapeDtypeStruct((T, QUERY_HEADS * D), bf16),
        in_specs=[SM] + [VM] * (len(parts) + 1),
        out_specs=VM,
        compiler_params=SMALL,
        cost_estimate=cost(1),
        name="out_q",
    )(idx, *parts, recv)


def along(x, distance):
    n = lax.axis_size("ctx")
    return lax.ppermute(x, "ctx", [(i, i + distance) for i in range(n) if 0 <= i + distance < n])


def swap(x, axis, bit):
    n = lax.axis_size(axis)
    return lax.ppermute(x, axis, [(i, i ^ bit) for i in range(n)])


def turned(x, chips):
    n = lax.axis_size("ctx")
    return lax.ppermute(x, "ctx", [(i, i // 16 * 16 + (i + 2 * chips) % 16) for i in range(n)])


def ends_kernel(x, y, dq_gain, dk_gain):
    dq_gain[...] = x[:1, :] + y[:1, :]
    dk_gain[...] = x[1:, :] + y[1:, :]


def ends(x, y):
    return pl.pallas_call(
        ends_kernel,
        out_shape=[jax.ShapeDtypeStruct((1, D), f32)] * 2,
        in_specs=[VM, VM],
        out_specs=[VM, VM],
        compiler_params=SMALL,
        cost_estimate=cost(0.1),
        name="ends",
    )(x, y)


def fold_kernel(gains, *rest):
    rest[-1][...] = jnp.sum(gains[...], axis=1)


def fold(gains, *after):
    return pl.pallas_call(
        fold_kernel,
        out_shape=jax.ShapeDtypeStruct((2, D), f32),
        in_specs=[VM] + [ANY] * len(after),
        out_specs=VM,
        compiler_params=SMALL,
        cost_estimate=cost(0.1),
        name="fold",
    )(gains, *after)


def plus_kernel(x, y, *rest):
    rest[-1][...] = x[...] + y[...]


def plus(x, y, *after):
    return pl.pallas_call(
        plus_kernel,
        out_shape=jax.ShapeDtypeStruct(x.shape, f32),
        in_specs=[VM, VM] + [ANY] * len(after),
        out_specs=VM,
        compiler_params=SMALL,
        cost_estimate=cost(0.1),
        name="plus",
    )(x, y, *after)


def on_device(q_raw, raw_keys_input, values, grad_out, q_gain, k_gain, doc_starts, flags):
    idx = lax.axis_index("ctx").astype(jnp.int32).reshape(1)
    q, k, v, do = q_raw[0], raw_keys_input[0], values[0], grad_out[0]
    qg, kg = q_gain.reshape(1, D), k_gain.reshape(1, D)
    count = len(CHUNKS)
    first = [sum(CHUNKS[:c]) for c in range(count)]

    keep, send = split_kv(idx, k, v)
    recv = swap(send, "ctx", 1)
    kv0, kv1, kv2 = [], [], []
    for c, n in enumerate(CHUNKS):
        kv0.append(join_kv(first[c], n, idx, keep, recv, kv1[c - 1 : c] if c >= 2 else []))
        kv1.append(along(kv0[c], 2))
    kv2 = [along(x, 2) for x in kv1]
    qa, doa = join_q(idx, q, do, swap(split_q(idx, q, do, kv0[0]), "ctx", 1))

    last = count - 1
    dqs, d0s, sums, r2s, gains = [], [], [], [], jnp.zeros((2, 8, D), f32)
    for c, n in enumerate(CHUNKS):
        after = kv1[c + 1 : c + 2]
        if c >= 2:
            after = after + [sums[c - 2]]
        if c >= 3:
            after = after + [r2s[c - 3]]
        dq, d2, d1, d0, gains = attn(
            first[c], n, idx, doc_starts, flags, qg, kg, gains, qa, doa, kv0[c], kv1[c], kv2[c], after
        )
        dqs.append(dq)
        d0s.append(d0)
        r1 = along(d2, -2)
        if c < last:
            sums.append(add_back(d1, r1))
            r2s.append(along(sums[c], -2))
    gain = fold(gains, sums[last - 1])
    gain = plus(gain, swap(gain, "ctx", 1))
    gain = plus(gain, turned(gain, 1))
    gain = plus(gain, turned(gain, 2))
    sums.append(add_back(d1, r1, gain))
    r2s.append(along(sums[last], -2))
    gain = plus(gain, swap(gain, "dp", 1), sums[last], *r2s[last - 2 : last - 1])
    gain = plus(gain, swap(gain, "dp", 4))
    gain = plus(gain, swap(gain, "dp", 2))
    steps = [gain]
    gain = plus(gain, swap(gain, "ctx", 16))
    steps.append(gain)
    dq_gain, dk_gain = ends(gain, turned(gain, 4))
    keeps, recvs = [], []
    for c, n in enumerate(CHUNKS):
        keep, send = finish(n, idx, kg, d0s[c], r2s[c], kv0[c], steps[c - count])
        keeps.append(keep)
        recvs.append(swap(send, "ctx", 1))
    dk, dv = out_kv(idx, keeps, recvs)
    dq = out_q(idx, dqs, swap(split_dq(idx, dqs), "ctx", 1))
    return dq[None], dk[None], dv[None], dq_gain.reshape(D), dk_gain.reshape(D)


def solution(mesh):
    in_specs = (
        P("dp", "ctx", None),
        P("dp", "ctx", None),
        P("dp", "ctx", None),
        P("dp", "ctx", None),
        P(),
        P(),
        P("dp", None),
        P("dp", None),
    )
    out_specs = (P("dp", "ctx", None), P("dp", "ctx", None), P("dp", "ctx", None), P(), P())
    return jax.shard_map(
        on_device, mesh=mesh, in_specs=in_specs, out_specs=out_specs, check_vma=False
    )
```
